32 devices in a mesh: wide: 8 (over z, y), narrow: 4 (over x, core).
Axes of the slice: x: 2, y: 2, z: 4, core: 2. Of those that a mesh axis runs over, the one named last changes fastest.
Arguments:
- parent_front: bfloat16 [3072, 5120], P('wide', 'narrow'), may hold values from -0.078125 to 0.078125
- child_updates: bfloat16 [2048, 2048], P('wide', 'narrow'), may hold values from -0.078125 to 0.078125
- child_map: int32 [2048], P('wide'), may hold values from 0 to 3071, as said below
- tile_mask: int32 [96, 40], P('wide', 'narrow'), may hold values 0 or 1
- probes: bfloat16 [5120, 512], P('narrow'), may hold values from -6 to 6
Outputs:
- probe_image: bfloat16 [3072, 512], P('wide', 'narrow')
The draws below stay inside these ranges and needn't reach their ends.
Inputs may be any that keep to these rules, and one draw needn't show every extreme that they name: `child_map`: the rows of one child go to distinct parent rows. Of the 256 rows of one child held by one wide device, exactly 32 have parent rows on each wide device w, that is rows w * 384 to (w + 1) * 384 - 1.
All inputs are finite; a program needn't handle non-finite values. No bound on the sum of `tile_mask` on one device may be relied on, other than what follows from the above.
Results may differ from the reference program's by a relative error of at most 0.012.
Values may be sent and summed in bfloat16 or wider, within the bound.
A program may use at most 128 MiB of HBM per device.

```python
import jax
import jax.numpy as jnp
from jax import lax

ROW_PAIR = 32
TOUCHED_DEV = 512
OWN_DEV = 768
PROBES = 512
TILE = 128
ROW_TILES = 12
CHILD_ROWS_DEV = 256
FRONT_ROWS_DEV = 384
ROW_TILE = 32
CHILD_ORDER = 1024
FRONT_ORDER = 3072
FRONT_COLS = 5120
CHILD_COLS = 2048
N_WIDE = 8
N_NARROW = 4


def draw_child_map(key, part):
    key = jax.random.fold_in(key, 11)
    wide_count = CHILD_ROWS_DEV // ROW_PAIR
    half_count = wide_count // 2
    key_list = jax.random.split(key, 2 * wide_count)
    chosen = jax.vmap(lambda single: jax.random.permutation(single, FRONT_ROWS_DEV)[:half_count * ROW_PAIR])(key_list)
    chosen = chosen.astype(jnp.int32).reshape(2, wide_count, half_count, ROW_PAIR)
    offsets = (jnp.arange(wide_count, dtype=jnp.int32) * FRONT_ROWS_DEV).reshape(1, wide_count, 1, 1)
    placed = (chosen + offsets).transpose(0, 2, 1, 3).reshape(2, half_count, wide_count * ROW_PAIR)
    shuffle_keys = jax.random.split(jax.random.fold_in(key, 1), 2 * half_count)
    shuffle = jax.vmap(lambda single: jax.random.permutation(single, wide_count * ROW_PAIR))(shuffle_keys)
    shuffle = shuffle.astype(jnp.int32).reshape(2, half_count, wide_count * ROW_PAIR)
    placed = jnp.take_along_axis(placed, shuffle, axis=2)
    return placed.reshape(-1).astype(jnp.int32)


def place_ends(entries, own_key, low, high):
    index_at = [jax.random.randint(jax.random.fold_in(own_key, axis), (), 0, length) for axis, length in enumerate(entries.shape)]
    widest = entries.shape.index(max(entries.shape))
    beside = index_at[:widest] + [(index_at[widest] + 1) % entries.shape[widest]] + index_at[widest + 1:]
    return entries.at[tuple(index_at)].set(low).at[tuple(beside)].set(high)


def level_of(key, extent, cuts, low, top_value):
    def one(dim, parts):
        steps = jax.random.uniform(jax.random.fold_in(jax.random.fold_in(key, 6), dim), (parts,), jnp.float32, low / len(cuts), top_value / len(cuts))
        return jnp.repeat(jnp.exp(steps), extent[dim] // parts).reshape((-1,) + (1,) * (len(extent) - dim - 1))

    loudness = one(*cuts[0])
    for cut in cuts[1:]:
        loudness = loudness * one(*cut)
    return loudness


def scatter_about(stream_key, dims, scale, reach, shards=(), held_as=jnp.bfloat16):
    level = level_of(stream_key, dims, shards, -0.22, 0.18) if shards else 1.0
    values = jax.random.normal(stream_key, dims, jnp.float32) * scale * level
    return jnp.minimum(jnp.maximum(values, -reach), reach).astype(held_as)


def setup_inputs(seed: int = 0) -> dict:
    arg_keys = jax.random.split(jax.random.key(seed), 6)
    parent_front = scatter_about(arg_keys[0], (FRONT_ORDER, FRONT_COLS), FRONT_COLS ** -0.5, 0.078125, ((0, 8), (1, 4)))
    child_updates = scatter_about(arg_keys[1], (2 * CHILD_ORDER, CHILD_COLS), FRONT_COLS ** -0.5, 0.078125, ((0, 8), (1, 4)))
    child_map = draw_child_map(jax.random.fold_in(arg_keys[5], 71), 0)
    tile_mask = place_ends((jax.random.randint(arg_keys[3], (FRONT_ORDER // ROW_TILE, FRONT_COLS // TILE), 0, 4) < 3).astype(jnp.int32), jax.random.fold_in(arg_keys[3], 1), 0, 1)
    probes = scatter_about(arg_keys[4], (FRONT_COLS, PROBES), 1.0, 6.0, ((0, 4),))
    return dict(parent_front=parent_front, child_updates=child_updates, child_map=child_map, tile_mask=tile_mask, probes=probes)


def masked_block(panel_block, mask_part):
    row_count, col_count = panel_block.shape
    tile_view = panel_block.reshape(mask_part.shape[0], row_count // mask_part.shape[0], mask_part.shape[1], col_count // mask_part.shape[1])
    return (tile_view * mask_part[:, None, :, None].astype(panel_block.dtype)).reshape(row_count, col_count)


def reference(parent_front, child_updates, child_map, tile_mask, probes):
    col_dev = TOUCHED_DEV + OWN_DEV
    child_three = child_updates.reshape(2 * CHILD_ORDER, N_NARROW, TOUCHED_DEV).astype(jnp.float32)
    added_sum = jnp.zeros((FRONT_ORDER, N_NARROW, TOUCHED_DEV), jnp.float32).at[child_map].add(child_three)
    parent_four = parent_front.reshape(N_WIDE, FRONT_ROWS_DEV, N_NARROW, col_dev)
    added_four = added_sum.reshape(N_WIDE, FRONT_ROWS_DEV, N_NARROW, TOUCHED_DEV)
    mask_four = tile_mask.reshape(N_WIDE, ROW_TILES, N_NARROW, col_dev // TILE)
    probe_three = probes.reshape(N_NARROW, col_dev, PROBES)

    def one_device(pieces):
        front_block, added_rows, mask_part = pieces
        summed = jnp.zeros((FRONT_ROWS_DEV, PROBES), jnp.float32)
        for group_index in range(N_NARROW):
            touched = (front_block[:, group_index, :TOUCHED_DEV].astype(jnp.float32) + added_rows[:, group_index]).astype(jnp.bfloat16)
            whole_panel = jnp.concatenate([touched, front_block[:, group_index, TOUCHED_DEV:]], axis=1)
            masked = masked_block(whole_panel, mask_part[:, group_index])
            partial_value = jnp.dot(masked, probe_three[group_index], preferred_element_type=jnp.float32).astype(jnp.bfloat16)
            summed = summed + lax.optimization_barrier(partial_value).astype(jnp.float32)
        return summed.astype(jnp.bfloat16)

    result = lax.map(one_device, (parent_four, added_four, mask_four))
    return result.reshape(FRONT_ORDER, PROBES)
```

```python
import functools

import jax
import jax.numpy as jnp
from jax import lax
from jax.experimental import pallas as pl
from jax.experimental.pallas import tpu as pltpu
from jax.sharding import PartitionSpec as P

TILE = 128
GROUP = 8
MESH = pl.DeviceIdType.MESH
F32 = jnp.float32
BF16 = jnp.bfloat16


def repeat(count, body):
    if count == 1:
        body(0)
    else:
        lax.fori_loop(0, count, lambda i, carry: (body(i), carry)[1], 0)


def iota(shape, dim):
    return lax.broadcasted_iota(jnp.int32, shape, dim)


def kernel(
    wide, narrow, per_peer, mask_rows,
    parent_in, child_in, map_in, mask_in, probes_in,
    out_ref,
    parent, child, cmap, mask, probes,
    mask_all, pick, sorted_rows, places_out, places_in, scaled,
    f_own, f_core, f_send, f_x,
    z_own, z_core, z_send, z_x, z_out, z_in,
    load_sem, mask_send, mask_recv, place_send, place_recv,
    z_out_send, z_in_recv, pair_send, pair_recv,
):
    rows, cols = parent.shape
    kids, touched = child.shape
    slots = GROUP * per_peer
    groups = wide // GROUP
    row_tile = rows // mask.shape[0]
    me_w = lax.axis_index("wide")
    me_n = lax.axis_index("narrow")
    core = lax.rem(me_n, 2)
    along = lax.div(me_n, 2)
    core_peer = (me_w, me_n + 1 - 2 * core)
    x_peer = (me_w, lax.rem(me_n + 2, narrow))

    def each_peer(fn):
        def one(k):
            fn(lax.rem(me_w + k, wide))

        if wide <= GROUP:
            for k in range(1, wide):
                one(k)
        else:
            lax.fori_loop(1, wide, lambda k, carry: (one(k), carry)[1], 0)

    loads = [
        pltpu.make_async_copy(src, dst, load_sem.at[i])
        for i, (src, dst) in enumerate(
            ((map_in, cmap), (mask_in, mask), (child_in, child), (probes_in, probes), (parent_in, parent))
        )
    ]
    for load in loads:
        load.start()

    barrier = pltpu.get_barrier_semaphore()
    each_peer(
        lambda w: pl.semaphore_signal(barrier, inc=1, device_id=(w, me_n), device_id_type=MESH)
    )
    for peer in (core_peer, x_peer):
        pl.semaphore_signal(barrier, inc=1, device_id=peer, device_id_type=MESH)

    def remote(src, dst, send, recv, device):
        return pltpu.make_async_remote_copy(
            src_ref=src, dst_ref=dst, send_sem=send, recv_sem=recv,
            device_id=device, device_id_type=MESH,
        )

    def block_at(index, size):
        return pl.ds(pl.multiple_of(index * size, size), size)

    loads[0].wait()
    child_rows = cmap[...]

    def order_group(g):
        first = g * GROUP
        low = (iota((2 * GROUP, 1), 0) + first) * rows
        chosen = (child_rows >= low) & (child_rows < low + rows)
        ones = jnp.where(chosen, 1.0, 0.0)
        before = []
        step = min(kids, 256)
        for start in range(0, kids, step):
            upper = iota((kids, step), 0) < iota((kids, step), 1) + start
            before.append(
                jnp.dot(
                    ones.astype(BF16),
                    jnp.where(upper, 1.0, 0.0).astype(BF16),
                    preferred_element_type=F32,
                )
            )
        rank = before[0] if len(before) == 1 else jnp.concatenate(before, axis=1)
        rank = jnp.where(chosen, rank, -1.0)
        wanted = iota((per_peer, kids), 0).astype(F32)
        base = jnp.zeros((1, kids), jnp.int32)
        for w in range(GROUP):
            here = rank[w : w + 1, :]
            pick[pl.ds(w * per_peer, per_peer), :] = jnp.where(here == wanted, 1.0, 0.0).astype(BF16)
            base = jnp.where(here >= 0.0, (first + w) * rows, base)
        local = child_rows - base
        high = (local >> 4).astype(F32)
        less = (local & 15).astype(F32)
        line = iota((TILE, kids), 0)
        coded = jnp.where(line == 0, high, jnp.where(line == 1, less, 0.0)).astype(BF16)
        places_out[block_at(g, slots), :] = lax.dot_general(
            pick[...], coded, (((1,), (1,)), ((), ())), preferred_element_type=F32
        ).astype(BF16)

    def sort_group(g):
        sorted_rows[block_at(g, slots), :] = jnp.dot(
            pick[...], child[...], preferred_element_type=F32
        ).astype(BF16)

    if groups == 1:
        order_group(0)
    else:
        loads[2].wait()

        def both(g):
            order_group(g)
            sort_group(g)

        repeat(groups, both)

    loads[1].wait()
    padded = jnp.zeros(mask_all.shape[1:], F32)
    mask_all[me_w] = padded.astype(BF16)
    mask_all[me_w, : mask.shape[0], : mask.shape[1]] = mask[...].astype(F32).astype(BF16)

    pl.semaphore_wait(barrier, wide + 1)

    def mask_copy(sender, w):
        return remote(
            mask_all.at[sender], mask_all.at[sender], mask_send.at[w], mask_recv.at[sender], (w, me_n)
        )

    def place_copy(sender, w):
        return remote(
            places_out.at[block_at(w, per_peer)],
            places_in.at[block_at(sender, per_peer)],
            place_send.at[w], place_recv.at[sender], (w, me_n),
        )

    each_peer(lambda w: mask_copy(me_w, w).start())
    each_peer(lambda w: place_copy(me_w, w).start())
    places_in[block_at(me_w, per_peer), :] = places_out[block_at(me_w, per_peer), :]

    if groups == 1:
        loads[2].wait()
        sort_group(0)

    loads[3].wait()
    loads[4].wait()
    part = 384 if rows % 384 == 0 else rows
    my_mask = mask_all[me_w]

    def parent_part(i):
        at = iota((part, mask_rows), 0) + i * part
        tile = iota((part, mask_rows), 1) * row_tile
        spread = jnp.where((at >= tile) & (at < tile + row_tile), 1.0, 0.0).astype(BF16)
        kept = jnp.dot(spread, my_mask, preferred_element_type=F32).astype(BF16)
        here = block_at(i, part)
        blocks = [
            parent[here, t * TILE : (t + 1) * TILE] * kept[:, t : t + 1]
            for t in range(cols // TILE)
        ]
        product = jnp.dot(
            jnp.concatenate(blocks, axis=1), probes[...], preferred_element_type=F32
        ).astype(BF16)
        for n in range(narrow):
            f_own[n % 2, n // 2, here, :] = product[:, n * TILE : (n + 1) * TILE]

    repeat(rows // part, parent_part)
    f_pair = remote(f_own.at[1 - core], f_core, pair_send.at[0], pair_recv.at[0], core_peer)
    f_pair.start()

    each_peer(lambda w: mask_copy(w, w).wait_recv())

    def child_group(g):
        here = block_at(g, slots)
        place = places_out[here, :].astype(F32)
        place = place[:, 0:1] * 16.0 + place[:, 1:2]
        lane = iota((slots, GROUP * mask_rows), 1)
        peer = iota((slots, GROUP * mask_rows), 0) >> (per_peer.bit_length() - 1)
        shift = mask_rows.bit_length() - 1
        tile = ((lane & (mask_rows - 1)) * row_tile).astype(F32)
        same = ((lane >> shift) == peer) & (place >= tile) & (place < tile + row_tile)
        table = mask_all[pl.ds(g * GROUP, GROUP)].reshape(GROUP * mask_rows, TILE)
        kept = jnp.dot(
            jnp.where(same, 1.0, 0.0).astype(BF16), table, preferred_element_type=F32
        ).astype(BF16)
        for t in range(touched // TILE):
            span = slice(t * TILE, (t + 1) * TILE)
            scaled[:, span] = sorted_rows[here, span] * kept[:, t : t + 1]
        product = jnp.dot(
            scaled[...], probes[:touched, :], preferred_element_type=F32
        ).astype(BF16)
        for n in range(narrow):
            z_own[n % 2, n // 2, here, :] = product[:, n * TILE : (n + 1) * TILE]

    repeat(groups, child_group)
    z_pair = remote(z_own.at[1 - core], z_core, pair_send.at[1], pair_recv.at[1], core_peer)
    z_pair.start()

    f_pair.wait_recv()
    f_send[...] = (f_own[core, 1 - along].astype(F32) + f_core[1 - along].astype(F32)).astype(BF16)
    z_pair.wait_recv()
    z_send[...] = (z_own[core, 1 - along].astype(F32) + z_core[1 - along].astype(F32)).astype(BF16)
    z_cross = remote(z_send, z_x, pair_send.at[2], pair_recv.at[2], x_peer)
    z_cross.start()
    f_cross = remote(f_send, f_x, pair_send.at[3], pair_recv.at[3], x_peer)
    f_cross.start()
    each_peer(lambda w: place_copy(w, w).wait_recv())
    z_cross.wait_recv()
    z_out[...] = (
        z_own[core, along].astype(F32) + z_core[along].astype(F32) + z_x[...].astype(F32)
    ).astype(BF16)

    def z_copy(sender, w):
        return remote(
            z_out.at[block_at(w, per_peer)],
            z_in.at[block_at(sender, per_peer)],
            z_out_send.at[w], z_in_recv.at[sender], (w, me_n),
        )

    each_peer(lambda w: z_copy(me_w, w).start())
    z_in[block_at(me_w, per_peer), :] = z_out[block_at(me_w, per_peer), :]

    f_cross.wait_recv()
    total = f_own[core, along].astype(F32) + f_core[along].astype(F32) + f_x[...].astype(F32)
    each_peer(lambda w: z_copy(w, w).wait_recv())
    for g in range(groups):
        place = places_in[g * slots : (g + 1) * slots, :].astype(F32)
        place = place[:, 0:1] * 16.0 + place[:, 1:2]
        lands = jnp.where(place == iota((slots, rows), 1).astype(F32), 1.0, 0.0).astype(BF16)
        total = total + lax.dot_general(
            lands, z_in[g * slots : (g + 1) * slots, :], (((0,), (0,)), ((), ())),
            preferred_element_type=F32,
        )
    out_ref[...] = total.astype(out_ref.dtype)

    each_peer(lambda w: mask_copy(me_w, w).wait_send())
    each_peer(lambda w: place_copy(me_w, w).wait_send())
    each_peer(lambda w: z_copy(me_w, w).wait_send())
    for copy in (f_pair, z_pair, z_cross, f_cross):
        copy.wait_send()


def local(wide, narrow, parent_front, child_updates, child_map, tile_mask, probes):
    rows, cols = parent_front.shape
    kids, touched = child_updates.shape
    per_peer = kids // wide
    probe_cols = probes.shape[1]
    mask_rows = 16 * pl.cdiv(tile_mask.shape[0], 16)
    vmem = pltpu.VMEM
    dma = pltpu.SemaphoreType.DMA
    return pl.pallas_call(
        functools.partial(kernel, wide, narrow, per_peer, mask_rows),
        out_shape=jax.ShapeDtypeStruct((rows, probe_cols // narrow), BF16),
        in_specs=[pl.BlockSpec(memory_space=pl.ANY)] * 5,
        out_specs=pl.BlockSpec(memory_space=pltpu.VMEM),
        scratch_shapes=[
            vmem((rows, cols), BF16),
            vmem((kids, touched), BF16),
            vmem((1, kids), jnp.int32),
            vmem(tile_mask.shape, jnp.int32),
            vmem(probes.shape, BF16),
            vmem((wide, mask_rows, TILE), BF16),
            vmem((GROUP * per_peer, kids), BF16),
            vmem((kids, touched), BF16),
            vmem((kids, TILE), BF16),
            vmem((kids, TILE), BF16),
            vmem((GROUP * per_peer, touched), BF16),
            vmem((2, 2, rows, TILE), BF16),
            vmem((2, rows, TILE), BF16),
            vmem((rows, TILE), BF16),
            vmem((rows, TILE), BF16),
            vmem((2, 2, kids, TILE), BF16),
            vmem((2, kids, TILE), BF16),
            vmem((kids, TILE), BF16),
            vmem((kids, TILE), BF16),
            vmem((kids, TILE), BF16),
            vmem((kids, TILE), BF16),
            dma((5,)),
            dma((wide,)),
            dma((wide,)),
            dma((wide,)),
            dma((wide,)),
            dma((wide,)),
            dma((wide,)),
            dma((4,)),
            dma((4,)),
        ],
        compiler_params=pltpu.CompilerParams(
            collective_id=0, has_side_effects=True, vmem_limit_bytes=56 * 1024 * 1024
        ),
    )(parent_front, child_updates, child_map.reshape(1, -1), tile_mask, probes)


def solution(mesh):
    placed = (
        P("wide", "narrow"),
        P("wide", "narrow"),
        P("wide"),
        P("wide", "narrow"),
        P("narrow", None),
    )
    return jax.shard_map(
        functools.partial(local, mesh.shape["wide"], mesh.shape["narrow"]),
        mesh=mesh, in_specs=placed, out_specs=P("wide", "narrow"), check_vma=False,
    )
```

```python
import functools

import jax
import jax.numpy as jnp
from jax import lax
from jax.experimental import pallas as pl
from jax.experimental.pallas import tpu as pltpu
from jax.sharding import PartitionSpec as P

TILE = 128
GROUP = 8
MESH = pl.DeviceIdType.MESH
F32 = jnp.float32
BF16 = jnp.bfloat16


def repeat(count, body):
    if count == 1:
        body(0)
    else:
        lax.fori_loop(0, count, lambda i, carry: (body(i), carry)[1], 0)


def iota(shape, dim):
    return lax.broadcasted_iota(jnp.int32, shape, dim)


def kernel(
    wide, narrow, per_peer, mask_rows,
    parent_in, child_in, map_in, mask_in, probes_in,
    out_ref,
    parent, child, cmap, mask, probes, mask_pad,
    msg_out, msg_in, pick, sorted_rows, lands,
    f_own, f_core, f_send, f_x,
    z_own, z_core, z_out, z_in,
    load_sem, msg_sem, z_sem, pair_send, pair_recv,
):
    rows, cols = parent.shape
    kids, touched = child.shape
    slots = GROUP * per_peer
    groups = wide // GROUP
    row_tile = rows // mask.shape[0]
    me_w = lax.axis_index("wide")
    me_n = lax.axis_index("narrow")
    core = lax.rem(me_n, 2)
    along = lax.div(me_n, 2)
    core_peer = (me_w, me_n + 1 - 2 * core)
    x_narrow = lax.rem(me_n + 2, narrow)
    x_peer = (me_w, x_narrow)

    def each_peer(fn, first=1):
        def one(k):
            fn(lax.rem(me_w + k, wide))

        if wide <= GROUP:
            for k in range(first, wide):
                one(k)
        else:
            lax.fori_loop(first, wide, lambda k, carry: (one(k), carry)[1], 0)

    def block_at(index, size):
        return pl.ds(pl.multiple_of(index * size, size), size)

    pairs = [(map_in, cmap), (mask_in, mask), (child_in, child), (parent_in, parent)]
    for n in range(narrow):
        pairs.append(
            (
                probes_in.at[:, n * TILE : (n + 1) * TILE],
                probes.at[n % 2, :, n // 2 * TILE : (n // 2 + 1) * TILE],
            )
        )
    loads = [
        pltpu.make_async_copy(src, dst, load_sem.at[i]) for i, (src, dst) in enumerate(pairs)
    ]
    for load in loads:
        load.start()

    barrier = pltpu.get_barrier_semaphore()

    def greet(device):
        pl.semaphore_signal(barrier, inc=1, device_id=device, device_id_type=MESH)

    greet(core_peer)
    each_peer(lambda w: greet((w, me_n)))
    each_peer(lambda w: greet((w, x_narrow)), first=0)

    def remote(src, dst, send, recv, device):
        return pltpu.make_async_remote_copy(
            src_ref=src, dst_ref=dst, send_sem=send, recv_sem=recv,
            device_id=device, device_id_type=MESH,
        )

    loads[0].wait()
    child_rows = cmap[...]

    def order_group(g):
        first = g * GROUP
        low = (iota((2 * GROUP, 1), 0) + first) * rows
        chosen = (child_rows >= low) & (child_rows < low + rows)
        ones = jnp.where(chosen, 1.0, 0.0)
        before = []
        step = min(kids, 256)
        for start in range(0, kids, step):
            upper = iota((kids, step), 0) < iota((kids, step), 1) + start
            before.append(
                jnp.dot(
                    ones.astype(BF16),
                    jnp.where(upper, 1.0, 0.0).astype(BF16),
                    preferred_element_type=F32,
                )
            )
        rank = before[0] if len(before) == 1 else jnp.concatenate(before, axis=1)
        rank = jnp.where(chosen, rank, -1.0)
        wanted = iota((per_peer, kids), 0).astype(F32)
        base = jnp.zeros((1, kids), jnp.int32)
        for w in range(GROUP):
            here = rank[w : w + 1, :]
            pick[pl.ds(w * per_peer, per_peer), :] = jnp.where(here == wanted, 1.0, 0.0).astype(BF16)
            base = jnp.where(here >= 0.0, (first + w) * rows, base)
        local = child_rows - base
        high = (local >> 4).astype(F32)
        less = (local & 15).astype(F32)
        line = iota((TILE, kids), 0)
        coded = jnp.where(line == 0, high, jnp.where(line == 1, less, 0.0)).astype(BF16)
        places = lax.dot_general(
            pick[...], coded, (((1,), (1,)), ((), ())), preferred_element_type=F32
        ).astype(BF16)
        msg_out[pl.ds(first, GROUP), :per_peer, :] = places.reshape(GROUP, per_peer, TILE)

    def sort_group(g):
        sorted_rows[block_at(g, slots), :] = jnp.dot(
            pick[...], child[...], preferred_element_type=F32
        ).astype(BF16)

    if groups == 1:
        order_group(0)
    else:
        loads[2].wait()

        def both(g):
            order_group(g)
            sort_group(g)

        repeat(groups, both)

    loads[1].wait()
    mask_pad[...] = jnp.zeros(mask_pad.shape, BF16)
    mask_pad[: mask.shape[0], : mask.shape[1]] = mask[...].astype(F32).astype(BF16)
    my_mask = mask_pad[...]
    repeat(groups, lambda g: msg_out.__setitem__(
        (pl.ds(g * GROUP, GROUP), slice(per_peer, per_peer + mask_rows)),
        jnp.broadcast_to(my_mask[None], (GROUP, mask_rows, TILE)),
    ))

    pl.semaphore_wait(barrier, 2 * wide)

    each_peer(
        lambda w: remote(
            msg_out.at[w], msg_in.at[me_w], msg_sem.at[0], msg_sem.at[1], (w, me_n)
        ).start()
    )
    msg_in[me_w] = msg_out[me_w]
    messages = remote(
        msg_out.at[pl.ds(0, wide - 1)], msg_in.at[pl.ds(0, wide - 1)],
        msg_sem.at[0], msg_sem.at[1], x_peer,
    )

    if groups == 1:
        loads[2].wait()
        sort_group(0)

    part = 384 if rows % 384 == 0 else rows

    def parent_mask(i):
        at = iota((part, mask_rows), 0) + i * part
        tile = iota((part, mask_rows), 1) * row_tile
        spread = jnp.where((at >= tile) & (at < tile + row_tile), 1.0, 0.0).astype(BF16)
        kept = jnp.dot(spread, my_mask, preferred_element_type=F32).astype(BF16)
        here = block_at(i, part)
        for t in range(cols // TILE):
            span = slice(t * TILE, (t + 1) * TILE)
            parent[here, span] = parent[here, span] * kept[:, t : t + 1]

    def parent_half(half):
        def one(i):
            product = jnp.dot(
                parent[block_at(i, part), :], probes[half], preferred_element_type=F32
            ).astype(BF16)
            for x in range(2):
                f_own[half, x, block_at(i, part), :] = product[:, x * TILE : (x + 1) * TILE]

        repeat(rows // part, one)

    loads[3].wait()
    repeat(rows // part, parent_mask)
    for load in loads[4:]:
        load.wait()
    parent_half(1 - core)
    f_pair = remote(f_own.at[1 - core], f_core, pair_send.at[0], pair_recv.at[0], core_peer)
    f_pair.start()
    parent_half(core)

    shift = mask_rows.bit_length() - 1

    def landing(g):
        place = msg_out[pl.ds(g * GROUP, GROUP), :per_peer, :].reshape(slots, TILE).astype(F32)
        place = place[:, 0:1] * 16.0 + place[:, 1:2]
        lane = iota((slots, GROUP * mask_rows), 1)
        peer = iota((slots, GROUP * mask_rows), 0) >> (per_peer.bit_length() - 1)
        tile = ((lane & (mask_rows - 1)) * row_tile).astype(F32)
        same = ((lane >> shift) == peer) & (place >= tile) & (place < tile + row_tile)
        return jnp.where(same, 1.0, 0.0).astype(BF16)

    def child_mask(g, tiles):
        table = msg_in[pl.ds(g * GROUP, GROUP), per_peer:, :].reshape(GROUP * mask_rows, TILE)
        kept = jnp.dot(tiles, table, preferred_element_type=F32).astype(BF16)
        here = block_at(g, slots)
        for t in range(touched // TILE):
            span = slice(t * TILE, (t + 1) * TILE)
            sorted_rows[here, span] = sorted_rows[here, span] * kept[:, t : t + 1]

    def child_half(half):
        def one(g):
            product = jnp.dot(
                sorted_rows[block_at(g, slots), :], probes[half, :touched, :],
                preferred_element_type=F32,
            ).astype(BF16)
            for x in range(2):
                z_own[half, x, block_at(g, slots), :] = product[:, x * TILE : (x + 1) * TILE]

        repeat(groups, one)

    if groups == 1:
        tiles = landing(0)
        messages.wait_recv()
        child_mask(0, tiles)
    else:
        messages.wait_recv()
        repeat(groups, lambda g: child_mask(g, landing(g)))
    child_half(1 - core)
    z_pair = remote(z_own.at[1 - core], z_core, pair_send.at[1], pair_recv.at[1], core_peer)
    z_pair.start()
    child_half(core)

    f_pair.wait_recv()
    f_send[...] = (f_own[core, 1 - along].astype(F32) + f_core[1 - along].astype(F32)).astype(BF16)
    f_cross = remote(f_send, f_x, pair_send.at[2], pair_recv.at[2], x_peer)
    f_cross.start()
    z_pair.wait_recv()

    def z_sum(x):
        z_out[block_at(x, kids), :] = (
            z_own[core, x].astype(F32) + z_core[x].astype(F32)
        ).astype(BF16)

    def z_start(x, n, w):
        remote(
            z_out.at[block_at(x * wide + w, per_peer)],
            z_in.at[block_at(along * wide + me_w, per_peer)],
            z_sem.at[0], z_sem.at[1], (w, n),
        ).start()

    z_sum(1 - along)
    each_peer(lambda w: z_start(1 - along, x_narrow, w), first=0)
    z_sum(along)
    each_peer(lambda w: z_start(along, me_n, w))
    mine = block_at(along * wide + me_w, per_peer)
    z_in[mine, :] = z_out[mine, :]
    most = pl.ds(0, (2 * wide - 1) * per_peer)
    arrivals = remote(z_out.at[most], z_in.at[most], z_sem.at[0], z_sem.at[1], x_peer)

    for g in range(groups):
        place = msg_in[g * GROUP : (g + 1) * GROUP, :per_peer, :].reshape(slots, TILE)
        lane = iota((2 * GROUP, TILE), 1)
        weigh = jnp.where(lane == 0, 16.0, jnp.where(lane == 1, 1.0, 0.0)).astype(BF16)
        place = lax.dot_general(
            weigh, place, (((1,), (1,)), ((), ())), preferred_element_type=F32
        )[0:1, :]
        lands[:, g * slots : (g + 1) * slots] = jnp.where(
            place == iota((rows, slots), 0).astype(F32), 1.0, 0.0
        ).astype(BF16)
    f_cross.wait_recv()
    total = f_own[core, along].astype(F32) + f_core[along].astype(F32) + f_x[...].astype(F32)
    arrivals.wait_recv()
    both_chips = jnp.concatenate([z_in[:kids, :], z_in[kids:, :]], axis=1)
    added = jnp.dot(lands[...], both_chips, preferred_element_type=F32)
    out_ref[...] = (total + (added[:, :TILE] + added[:, TILE:])).astype(out_ref.dtype)

    messages.wait_send()
    arrivals.wait_send()
    for copy in (f_pair, z_pair, f_cross):
        copy.wait_send()


def local(wide, narrow, parent_front, child_updates, child_map, tile_mask, probes):
    rows, cols = parent_front.shape
    kids, touched = child_updates.shape
    per_peer = kids // wide
    probe_cols = probes.shape[1]
    mask_rows = 16 * pl.cdiv(tile_mask.shape[0], 16)
    shapes = [
        ((rows, cols), BF16),
        ((kids, touched), BF16),
        ((1, kids), jnp.int32),
        (tile_mask.shape, jnp.int32),
        ((2, cols, 2 * TILE), BF16),
        ((mask_rows, TILE), BF16),
        ((wide, per_peer + mask_rows, TILE), BF16),
        ((wide, per_peer + mask_rows, TILE), BF16),
        ((GROUP * per_peer, kids), BF16),
        ((kids, touched), BF16),
        ((rows, kids), BF16),
        ((2, 2, rows, TILE), BF16),
        ((2, rows, TILE), BF16),
        ((rows, TILE), BF16),
        ((rows, TILE), BF16),
        ((2, 2, kids, TILE), BF16),
        ((2, kids, TILE), BF16),
        ((2 * kids, TILE), BF16),
        ((2 * kids, TILE), BF16),
    ]
    dma = pltpu.SemaphoreType.DMA
    return pl.pallas_call(
        functools.partial(kernel, wide, narrow, per_peer, mask_rows),
        out_shape=jax.ShapeDtypeStruct((rows, probe_cols // narrow), BF16),
        in_specs=[pl.BlockSpec(memory_space=pltpu.HBM)] * 5,
        out_specs=pl.BlockSpec(memory_space=pltpu.VMEM),
        scratch_shapes=[pltpu.VMEM(shape, dtype) for shape, dtype in shapes]
        + [dma((8,)), dma((2,)), dma((2,)), dma((3,)), dma((3,))],
        compiler_params=pltpu.CompilerParams(
            collective_id=0, has_side_effects=True,
            vmem_limit_bytes=56 * 1024 * 1024,
        ),
    )(parent_front, child_updates, child_map.reshape(1, -1), tile_mask, probes)


def solution(mesh):
    placed = (
        P("wide", "narrow"),
        P("wide", "narrow"),
        P("wide"),
        P("wide", "narrow"),
        P("narrow", None),
    )
    return jax.shard_map(
        functools.partial(local, mesh.shape["wide"], mesh.shape["narrow"]),
        mesh=mesh, in_specs=placed, out_specs=P("wide", "narrow"), check_vma=False,
    )
```

```python
import functools

import jax
import jax.numpy as jnp
from jax import lax
from jax.experimental import pallas as pl
from jax.experimental.pallas import tpu as pltpu
from jax.sharding import PartitionSpec as P

TILE = 128
GROUP = 8
MESH = pl.DeviceIdType.MESH
F32 = jnp.float32
BF16 = jnp.bfloat16


def repeat(count, body):
    if count == 1:
        body(0)
    else:
        lax.fori_loop(0, count, lambda i, carry: (body(i), carry)[1], 0)


def iota(shape, dim):
    return lax.broadcasted_iota(jnp.int32, shape, dim)


def kernel(
    wide, narrow, per_peer, mask_rows,
    parent_in, child_in, map_in, mask_in, probes_in,
    out_ref,
    parent, child, cmap, mask, probes, mask_pad,
    msg_out, msg_in, pick, sorted_rows, lands,
    f_own, f_core, f_send, f_x,
    z_own, z_core, z_out, z_in,
    load_sem, msg_sem, z_sem, pair_send, pair_recv, ready,
):
    rows, cols = parent.shape
    kids, touched = child.shape
    slots = GROUP * per_peer
    groups = wide // GROUP
    row_tile = rows // mask.shape[0]
    me_w = lax.axis_index("wide")
    me_n = lax.axis_index("narrow")
    core = lax.rem(me_n, 2)
    along = lax.div(me_n, 2)
    core_peer = (me_w, me_n + 1 - 2 * core)
    x_narrow = lax.rem(me_n + 2, narrow)
    x_peer = (me_w, x_narrow)

    def each_peer(fn, first=1):
        def one(k):
            fn(lax.rem(me_w + k, wide))

        if wide <= GROUP:
            for k in range(first, wide):
                one(k)
        else:
            lax.fori_loop(first, wide, lambda k, carry: (one(k), carry)[1], 0)

    def block_at(index, size):
        return pl.ds(pl.multiple_of(index * size, size), size)

    barrier = pltpu.get_barrier_semaphore()

    def greet(device):
        pl.semaphore_signal(barrier, inc=1, device_id=device, device_id_type=MESH)

    each_peer(lambda w: greet((w, me_n)))
    greet(core_peer)
    greet(x_peer)

    pairs = [(map_in, cmap), (mask_in, mask), (child_in, child), (parent_in, parent)]
    for n in range(narrow):
        pairs.append(
            (
                probes_in.at[:, n * TILE : (n + 1) * TILE],
                probes.at[n % 2, :, n // 2 * TILE : (n // 2 + 1) * TILE],
            )
        )
    loads = [
        pltpu.make_async_copy(src, dst, load_sem.at[i]) for i, (src, dst) in enumerate(pairs)
    ]
    for load in loads:
        load.start()

    def remote(src, dst, send, recv, device):
        return pltpu.make_async_remote_copy(
            src_ref=src, dst_ref=dst, send_sem=send, recv_sem=recv,
            device_id=device, device_id_type=MESH,
        )

    loads[0].wait()
    child_rows = cmap[...]

    def order_group(g):
        first = g * GROUP
        low = (iota((2 * GROUP, 1), 0) + first) * rows
        chosen = (child_rows >= low) & (child_rows < low + rows)
        ones = jnp.where(chosen, 1.0, 0.0)
        before = []
        step = min(kids, 256)
        for start in range(0, kids, step):
            upper = iota((kids, step), 0) < iota((kids, step), 1) + start
            before.append(
                jnp.dot(
                    ones.astype(BF16),
                    jnp.where(upper, 1.0, 0.0).astype(BF16),
                    preferred_element_type=F32,
                )
            )
        rank = before[0] if len(before) == 1 else jnp.concatenate(before, axis=1)
        rank = jnp.where(chosen, rank, -1.0)
        wanted = iota((per_peer, kids), 0).astype(F32)
        base = jnp.zeros((1, kids), jnp.int32)
        for w in range(GROUP):
            here = rank[w : w + 1, :]
            pick[pl.ds(w * per_peer, per_peer), :] = jnp.where(here == wanted, 1.0, 0.0).astype(BF16)
            base = jnp.where(here >= 0.0, (first + w) * rows, base)
        local = child_rows - base
        high = (local >> 4).astype(F32)
        less = (local & 15).astype(F32)
        line = iota((TILE, kids), 0)
        coded = jnp.where(line == 0, high, jnp.where(line == 1, less, 0.0)).astype(BF16)
        places = lax.dot_general(
            pick[...], coded, (((1,), (1,)), ((), ())), preferred_element_type=F32
        ).astype(BF16)
        msg_out[pl.ds(first, GROUP), :per_peer, :] = places.reshape(GROUP, per_peer, TILE)

    def sort_group(g):
        sorted_rows[block_at(g, slots), :] = jnp.dot(
            pick[...], child[...], preferred_element_type=F32
        ).astype(BF16)

    if groups == 1:
        order_group(0)
    else:
        loads[2].wait()

        def both(g):
            order_group(g)
            sort_group(g)

        repeat(groups, both)

    loads[1].wait()
    mask_pad[...] = jnp.zeros(mask_pad.shape, BF16)
    mask_pad[: mask.shape[0], : mask.shape[1]] = mask[...].astype(F32).astype(BF16)
    my_mask = mask_pad[...]
    repeat(groups, lambda g: msg_out.__setitem__(
        (pl.ds(g * GROUP, GROUP), slice(per_peer, per_peer + mask_rows)),
        jnp.broadcast_to(my_mask[None], (GROUP, mask_rows, TILE)),
    ))

    pl.semaphore_wait(barrier, wide + 1)

    each_peer(
        lambda w: remote(
            msg_out.at[w], msg_in.at[me_w], msg_sem.at[0], msg_sem.at[1], (w, me_n)
        ).start()
    )
    msg_in[me_w] = msg_out[me_w]
    messages = remote(
        msg_out.at[pl.ds(0, wide - 1)], msg_in.at[pl.ds(0, wide - 1)],
        msg_sem.at[0], msg_sem.at[1], x_peer,
    )

    if groups == 1:
        loads[2].wait()
        sort_group(0)

    part = 384 if rows % 384 == 0 else rows

    def parent_mask(i):
        at = iota((part, mask_rows), 0) + i * part
        tile = iota((part, mask_rows), 1) * row_tile
        spread = jnp.where((at >= tile) & (at < tile + row_tile), 1.0, 0.0).astype(BF16)
        kept = jnp.dot(spread, my_mask, preferred_element_type=F32).astype(BF16)
        here = block_at(i, part)
        for t in range(cols // TILE):
            span = slice(t * TILE, (t + 1) * TILE)
            parent[here, span] = parent[here, span] * kept[:, t : t + 1]

    def parent_half(half):
        def one(i):
            product = jnp.dot(
                parent[block_at(i, part), :], probes[half], preferred_element_type=F32
            ).astype(BF16)
            for x in range(2):
                f_own[half, x, block_at(i, part), :] = product[:, x * TILE : (x + 1) * TILE]

        repeat(rows // part, one)

    loads[3].wait()
    repeat(rows // part, parent_mask)
    for load in loads[4:]:
        load.wait()
    parent_half(1 - core)
    f_pair = remote(f_own.at[1 - core], f_core, pair_send.at[0], pair_recv.at[0], core_peer)
    f_pair.start()

    shift = mask_rows.bit_length() - 1

    def landing(g):
        place = msg_out[pl.ds(g * GROUP, GROUP), :per_peer, :].reshape(slots, TILE).astype(F32)
        place = place[:, 0:1] * 16.0 + place[:, 1:2]
        lane = iota((slots, GROUP * mask_rows), 1)
        peer = iota((slots, GROUP * mask_rows), 0) >> (per_peer.bit_length() - 1)
        tile = ((lane & (mask_rows - 1)) * row_tile).astype(F32)
        same = ((lane >> shift) == peer) & (place >= tile) & (place < tile + row_tile)
        return jnp.where(same, 1.0, 0.0).astype(BF16)

    def child_mask(g, tiles):
        table = msg_in[pl.ds(g * GROUP, GROUP), per_peer:, :].reshape(GROUP * mask_rows, TILE)
        kept = jnp.dot(tiles, table, preferred_element_type=F32).astype(BF16)
        here = block_at(g, slots)
        for t in range(touched // TILE):
            span = slice(t * TILE, (t + 1) * TILE)
            sorted_rows[here, span] = sorted_rows[here, span] * kept[:, t : t + 1]

    def child_half(half):
        def one(g):
            product = jnp.dot(
                sorted_rows[block_at(g, slots), :], probes[half, :touched, :],
                preferred_element_type=F32,
            ).astype(BF16)
            for x in range(2):
                z_own[half, x, block_at(g, slots), :] = product[:, x * TILE : (x + 1) * TILE]

        repeat(groups, one)

    def all_in():
        messages.wait_recv()
        pl.semaphore_signal(ready, inc=1, device_id=x_peer, device_id_type=MESH)

    if groups == 1:
        tiles = landing(0)
        all_in()
        child_mask(0, tiles)
    else:
        all_in()
        repeat(groups, lambda g: child_mask(g, landing(g)))
    child_half(1 - core)
    z_pair = remote(z_own.at[1 - core], z_core, pair_send.at[1], pair_recv.at[1], core_peer)
    z_pair.start()
    child_half(core)
    parent_half(core)

    f_pair.wait_recv()
    f_send[...] = (f_own[core, 1 - along].astype(F32) + f_core[1 - along].astype(F32)).astype(BF16)
    f_cross = remote(f_send, f_x, pair_send.at[2], pair_recv.at[2], x_peer)
    f_cross.start()
    z_pair.wait_recv()

    def z_sum(x):
        z_out[block_at(x, kids), :] = (
            z_own[core, x].astype(F32) + z_core[x].astype(F32)
        ).astype(BF16)

    def z_start(x, n, w):
        remote(
            z_out.at[block_at(x * wide + w, per_peer)],
            z_in.at[block_at(along * wide + me_w, per_peer)],
            z_sem.at[0], z_sem.at[1], (w, n),
        ).start()

    z_sum(1 - along)
    pl.semaphore_wait(ready, 1)
    each_peer(lambda w: z_start(1 - along, x_narrow, w), first=0)
    z_sum(along)
    each_peer(lambda w: z_start(along, me_n, w))
    mine = block_at(along * wide + me_w, per_peer)
    z_in[mine, :] = z_out[mine, :]
    most = pl.ds(0, (2 * wide - 1) * per_peer)
    arrivals = remote(z_out.at[most], z_in.at[most], z_sem.at[0], z_sem.at[1], x_peer)

    for g in range(groups):
        place = msg_in[g * GROUP : (g + 1) * GROUP, :per_peer, :].reshape(slots, TILE)
        lane = iota((2 * GROUP, TILE), 1)
        weigh = jnp.where(lane == 0, 16.0, jnp.where(lane == 1, 1.0, 0.0)).astype(BF16)
        place = lax.dot_general(
            weigh, place, (((1,), (1,)), ((), ())), preferred_element_type=F32
        )[0:1, :]
        lands[:, g * slots : (g + 1) * slots] = jnp.where(
            place == iota((rows, slots), 0).astype(F32), 1.0, 0.0
        ).astype(BF16)
    f_cross.wait_recv()
    total = f_own[core, along].astype(F32) + f_core[along].astype(F32) + f_x[...].astype(F32)
    arrivals.wait_recv()
    both_chips = jnp.concatenate([z_in[:kids, :], z_in[kids:, :]], axis=1)
    added = jnp.dot(lands[...], both_chips, preferred_element_type=F32)
    out_ref[...] = (total + (added[:, :TILE] + added[:, TILE:])).astype(out_ref.dtype)

    messages.wait_send()
    arrivals.wait_send()
    for copy in (f_pair, z_pair, f_cross):
        copy.wait_send()


def local(wide, narrow, parent_front, child_updates, child_map, tile_mask, probes):
    rows, cols = parent_front.shape
    kids, touched = child_updates.shape
    per_peer = kids // wide
    probe_cols = probes.shape[1]
    mask_rows = 16 * pl.cdiv(tile_mask.shape[0], 16)
    shapes = [
        ((rows, cols), BF16),
        ((kids, touched), BF16),
        ((1, kids), jnp.int32),
        (tile_mask.shape, jnp.int32),
        ((2, cols, 2 * TILE), BF16),
        ((mask_rows, TILE), BF16),
        ((wide, per_peer + mask_rows, TILE), BF16),
        ((wide, per_peer + mask_rows, TILE), BF16),
        ((GROUP * per_peer, kids), BF16),
        ((kids, touched), BF16),
        ((rows, kids), BF16),
        ((2, 2, rows, TILE), BF16),
        ((2, rows, TILE), BF16),
        ((rows, TILE), BF16),
        ((rows, TILE), BF16),
        ((2, 2, kids, TILE), BF16),
        ((2, kids, TILE), BF16),
        ((2 * kids, TILE), BF16),
        ((2 * kids, TILE), BF16),
    ]
    dma = pltpu.SemaphoreType.DMA
    return pl.pallas_call(
        functools.partial(kernel, wide, narrow, per_peer, mask_rows),
        out_shape=pltpu.VMEM((rows, probe_cols // narrow), BF16),
        in_specs=[pl.BlockSpec(memory_space=pltpu.HBM)] * 5,
        out_specs=pl.BlockSpec(memory_space=pltpu.VMEM),
        scratch_shapes=[pltpu.VMEM(shape, dtype) for shape, dtype in shapes]
        + [dma((8,)), dma((2,)), dma((2,)), dma((3,)), dma((3,)), pltpu.SemaphoreType.REGULAR],
        compiler_params=pltpu.CompilerParams(
            collective_id=0, has_side_effects=True,
            vmem_limit_bytes=56 * 1024 * 1024,
        ),
    )(parent_front, child_updates, child_map.reshape(1, -1), tile_mask, probes)


def solution(mesh):
    placed = (
        P("wide", "narrow"),
        P("wide", "narrow"),
        P("wide"),
        P("wide", "narrow"),
        P("narrow", None),
    )
    return jax.shard_map(
        functools.partial(local, mesh.shape["wide"], mesh.shape["narrow"]),
        mesh=mesh, in_specs=placed, out_specs=P("wide", "narrow"), check_vma=False,
    )
```

```python
import functools

import jax
import jax.numpy as jnp
from jax import lax
from jax.experimental import pallas as pl
from jax.experimental.pallas import tpu as pltpu
from jax.sharding import PartitionSpec as P

TILE = 128
GROUP = 8
MESH = pl.DeviceIdType.MESH
F32 = jnp.float32
BF16 = jnp.bfloat16


def repeat(count, body):
    if count == 1:
        body(0)
    else:
        lax.fori_loop(0, count, lambda i, carry: (body(i), carry)[1], 0)


def iota(shape, dim):
    return lax.broadcasted_iota(jnp.int32, shape, dim)


def kernel(
    wide, narrow, per_peer, mask_rows,
    parent_in, child_in, map_in, mask_in, probes_in,
    out_ref,
    parent, child, cmap, mask, probes, mask_pad,
    probes_far, msg_out, msg_in, mask_far, pick, sorted_rows, lands,
    f_own, f_core, f_send, f_x,
    z_out, z_in,
    load_sem, msg_sem, far_sem, z_sem, pair_send, pair_recv, ready,
):
    rows, cols = parent.shape
    _, kids, touched = child.shape
    slots = GROUP * per_peer
    groups = wide // GROUP
    row_tile = rows // mask.shape[0]
    me_w = lax.axis_index("wide")
    me_n = lax.axis_index("narrow")
    core = lax.rem(me_n, 2)
    along = lax.div(me_n, 2)
    core_narrow = me_n + 1 - 2 * core
    core_peer = (me_w, core_narrow)
    x_narrow = lax.rem(me_n + 2, narrow)
    x_peer = (me_w, x_narrow)

    def each_peer(fn, first=1):
        def one(k):
            fn(lax.rem(me_w + k, wide))

        if wide <= GROUP:
            for k in range(first, wide):
                one(k)
        else:
            lax.fori_loop(first, wide, lambda k, carry: (one(k), carry)[1], 0)

    def block_at(index, size):
        return pl.ds(pl.multiple_of(index * size, size), size)

    barrier = pltpu.get_barrier_semaphore()

    def greet(device):
        pl.semaphore_signal(barrier, inc=1, device_id=device, device_id_type=MESH)

    each_peer(lambda w: greet((w, me_n)))
    each_peer(lambda w: greet((w, core_narrow)), first=0)
    greet(x_peer)

    pairs = [(map_in, cmap), (mask_in, mask), (child_in, child.at[0]), (parent_in, parent)]
    for n in range(narrow):
        pairs.append(
            (
                probes_in.at[:, n * TILE : (n + 1) * TILE],
                probes.at[n % 2, :, n // 2 * TILE : (n // 2 + 1) * TILE],
            )
        )
    loads = [
        pltpu.make_async_copy(src, dst, load_sem.at[i]) for i, (src, dst) in enumerate(pairs)
    ]
    for load in loads:
        load.start()

    def remote(src, dst, send, recv, device):
        return pltpu.make_async_remote_copy(
            src_ref=src, dst_ref=dst, send_sem=send, recv_sem=recv,
            device_id=device, device_id_type=MESH,
        )

    loads[0].wait()
    child_rows = cmap[...]

    def order_group(g):
        first = g * GROUP
        low = (iota((2 * GROUP, 1), 0) + first) * rows
        chosen = (child_rows >= low) & (child_rows < low + rows)
        ones = jnp.where(chosen, 1.0, 0.0)
        before = []
        step = min(kids, 256)
        for start in range(0, kids, step):
            upper = iota((kids, step), 0) < iota((kids, step), 1) + start
            before.append(
                jnp.dot(
                    ones.astype(BF16),
                    jnp.where(upper, 1.0, 0.0).astype(BF16),
                    preferred_element_type=F32,
                )
            )
        rank = before[0] if len(before) == 1 else jnp.concatenate(before, axis=1)
        rank = jnp.where(chosen, rank, -1.0)
        wanted = iota((per_peer, kids), 0).astype(F32)
        base = jnp.zeros((1, kids), jnp.int32)
        for w in range(GROUP):
            here = rank[w : w + 1, :]
            pick[block_at(first + w, per_peer), :] = jnp.where(here == wanted, 1.0, 0.0).astype(BF16)
            base = jnp.where(here >= 0.0, (first + w) * rows, base)
        local = child_rows - base
        high = (local >> 4).astype(F32)
        less = (local & 15).astype(F32)
        line = iota((TILE, kids), 0)
        coded = jnp.where(line == 0, high, jnp.where(line == 1, less, 0.0)).astype(BF16)
        places = lax.dot_general(
            pick[block_at(g, slots), :], coded, (((1,), (1,)), ((), ())), preferred_element_type=F32
        ).astype(BF16)
        msg_out[pl.ds(first, GROUP), :per_peer, :] = places.reshape(GROUP, per_peer, TILE)

    def sort_group(g, source):
        sorted_rows[block_at(g, slots), source * touched : (source + 1) * touched] = jnp.dot(
            pick[block_at(g, slots), :], child[source], preferred_element_type=F32
        ).astype(BF16)

    repeat(groups, order_group)

    loads[1].wait()
    mask_pad[...] = jnp.zeros(mask_pad.shape, BF16)
    mask_pad[: mask.shape[0], : mask.shape[1]] = mask[...].astype(F32).astype(BF16)
    my_mask = mask_pad[...]
    repeat(groups, lambda g: msg_out.__setitem__(
        (pl.ds(g * GROUP, GROUP), slice(per_peer, per_peer + mask_rows)),
        jnp.broadcast_to(my_mask[None], (GROUP, mask_rows, TILE)),
    ))

    pl.semaphore_wait(barrier, 2 * wide)

    far_copies = [remote(child_in, child.at[1], far_sem.at[0], far_sem.at[1], core_peer)]
    for x in range(2):
        span = pl.ds(pl.multiple_of((2 * x + 1 - core) * TILE, TILE), TILE)
        far_copies.append(
            remote(
                probes_in.at[:touched, span], probes_far.at[:, x * TILE : (x + 1) * TILE],
                far_sem.at[2 + 2 * x], far_sem.at[3 + 2 * x], core_peer,
            )
        )

    each_peer(
        lambda w: remote(
            msg_out.at[w], msg_in.at[me_w], msg_sem.at[0], msg_sem.at[1], (w, me_n)
        ).start()
    )
    for copy in far_copies:
        copy.start()
    each_peer(
        lambda w: remote(
            mask_pad, mask_far.at[me_w], msg_sem.at[2], msg_sem.at[3], (w, core_narrow)
        ).start(),
        first=0,
    )
    msg_in[me_w] = msg_out[me_w]
    masks = remote(mask_far, mask_far, msg_sem.at[2], msg_sem.at[3], core_peer)
    messages = remote(
        msg_out.at[pl.ds(0, wide - 1)], msg_in.at[pl.ds(0, wide - 1)],
        msg_sem.at[0], msg_sem.at[1], x_peer,
    )

    loads[2].wait()
    repeat(groups, lambda g: sort_group(g, 0))

    part = 384 if rows % 384 == 0 else rows

    def parent_mask(i):
        at = iota((part, mask_rows), 0) + i * part
        tile = iota((part, mask_rows), 1) * row_tile
        spread = jnp.where((at >= tile) & (at < tile + row_tile), 1.0, 0.0).astype(BF16)
        kept = jnp.dot(spread, my_mask, preferred_element_type=F32).astype(BF16)
        here = block_at(i, part)
        for t in range(cols // TILE):
            span = slice(t * TILE, (t + 1) * TILE)
            parent[here, span] = parent[here, span] * kept[:, t : t + 1]

    def parent_half(half):
        def one(i):
            product = jnp.dot(
                parent[block_at(i, part), :], probes[half], preferred_element_type=F32
            ).astype(BF16)
            for x in range(2):
                f_own[half, x, block_at(i, part), :] = product[:, x * TILE : (x + 1) * TILE]

        repeat(rows // part, one)

    loads[3].wait()
    repeat(rows // part, parent_mask)
    for load in loads[4:]:
        load.wait()
    parent_half(1 - core)
    f_pair = remote(f_own.at[1 - core], f_core, pair_send.at[0], pair_recv.at[0], core_peer)
    f_pair.start()
    parent_half(core)
    far_copies[0].wait_recv()
    repeat(groups, lambda g: sort_group(g, 1))

    shift = mask_rows.bit_length() - 1

    def landing(g):
        place = msg_out[pl.ds(g * GROUP, GROUP), :per_peer, :].reshape(slots, TILE).astype(F32)
        place = place[:, 0:1] * 16.0 + place[:, 1:2]
        lane = iota((slots, GROUP * mask_rows), 1)
        peer = iota((slots, GROUP * mask_rows), 0) >> (per_peer.bit_length() - 1)
        tile = ((lane & (mask_rows - 1)) * row_tile).astype(F32)
        same = ((lane >> shift) == peer) & (place >= tile) & (place < tile + row_tile)
        return jnp.where(same, 1.0, 0.0).astype(BF16)

    def child_mask(g, tiles):
        table = msg_in[pl.ds(g * GROUP, GROUP), per_peer:, :].reshape(GROUP * mask_rows, TILE)
        far = mask_far[pl.ds(g * GROUP, GROUP)].reshape(GROUP * mask_rows, TILE)
        here = block_at(g, slots)
        count = touched // TILE
        for source, part_table in enumerate((table, far)):
            kept = jnp.dot(tiles, part_table, preferred_element_type=F32).astype(BF16)
            for t in range(count):
                span = slice((source * count + t) * TILE, (source * count + t + 1) * TILE)
                sorted_rows[here, span] = sorted_rows[here, span] * kept[:, t : t + 1]

    def child_product(g):
        here = block_at(g, slots)
        product = jnp.dot(
            sorted_rows[here, :touched], probes[core, :touched, :], preferred_element_type=F32
        ) + jnp.dot(sorted_rows[here, touched:], probes_far[...], preferred_element_type=F32)
        product = product.astype(BF16)
        for x in range(2):
            z_out[block_at(x * groups + g, slots), :] = product[:, x * TILE : (x + 1) * TILE]

    f_pair.wait_recv()
    f_send[...] = (f_own[core, 1 - along].astype(F32) + f_core[1 - along].astype(F32)).astype(BF16)
    f_cross = remote(f_send, f_x, pair_send.at[1], pair_recv.at[1], x_peer)
    f_cross.start()

    def all_in():
        messages.wait_recv()
        pl.semaphore_signal(ready, inc=1, device_id=x_peer, device_id_type=MESH)
        masks.wait_recv()

    if groups == 1:
        tiles = landing(0)
        all_in()
        child_mask(0, tiles)
    else:
        all_in()
        repeat(groups, lambda g: child_mask(g, landing(g)))
    for copy in far_copies[1:]:
        copy.wait_recv()
    repeat(groups, child_product)

    def z_start(x, n, w):
        remote(
            z_out.at[block_at(x * wide + w, per_peer)],
            z_in.at[block_at(along * wide + me_w, per_peer)],
            z_sem.at[0], z_sem.at[1], (w, n),
        ).start()

    pl.semaphore_wait(ready, 1)
    each_peer(lambda w: z_start(1 - along, x_narrow, w), first=0)
    each_peer(lambda w: z_start(along, me_n, w))
    mine = block_at(along * wide + me_w, per_peer)
    z_in[mine, :] = z_out[mine, :]
    most = pl.ds(0, (2 * wide - 1) * per_peer)
    arrivals = remote(z_out.at[most], z_in.at[most], z_sem.at[0], z_sem.at[1], x_peer)

    for g in range(groups):
        place = msg_in[g * GROUP : (g + 1) * GROUP, :per_peer, :].reshape(slots, TILE)
        lane = iota((2 * GROUP, TILE), 1)
        weigh = jnp.where(lane == 0, 16.0, jnp.where(lane == 1, 1.0, 0.0)).astype(BF16)
        place = lax.dot_general(
            weigh, place, (((1,), (1,)), ((), ())), preferred_element_type=F32
        )[0:1, :]
        lands[:, g * slots : (g + 1) * slots] = jnp.where(
            place == iota((rows, slots), 0).astype(F32), 1.0, 0.0
        ).astype(BF16)
    f_cross.wait_recv()
    total = f_own[core, along].astype(F32) + f_core[along].astype(F32) + f_x[...].astype(F32)
    arrivals.wait_recv()
    both_chips = jnp.concatenate([z_in[:kids, :], z_in[kids:, :]], axis=1)
    added = jnp.dot(lands[...], both_chips, preferred_element_type=F32)
    out_ref[...] = (total + (added[:, :TILE] + added[:, TILE:])).astype(out_ref.dtype)

    messages.wait_send()
    masks.wait_send()
    arrivals.wait_send()
    for copy in (f_pair, f_cross, *far_copies):
        copy.wait_send()


def local(wide, narrow, parent_front, child_updates, child_map, tile_mask, probes):
    rows, cols = parent_front.shape
    kids, touched = child_updates.shape
    per_peer = kids // wide
    probe_cols = probes.shape[1]
    mask_rows = 16 * pl.cdiv(tile_mask.shape[0], 16)
    shapes = [
        ((rows, cols), BF16),
        ((2, kids, touched), BF16),
        ((1, kids), jnp.int32),
        (tile_mask.shape, jnp.int32),
        ((2, cols, 2 * TILE), BF16),
        ((mask_rows, TILE), BF16),
        ((touched, 2 * TILE), BF16),
        ((wide, per_peer + mask_rows, TILE), BF16),
        ((wide, per_peer + mask_rows, TILE), BF16),
        ((wide, mask_rows, TILE), BF16),
        ((kids, kids), BF16),
        ((kids, 2 * touched), BF16),
        ((rows, kids), BF16),
        ((2, 2, rows, TILE), BF16),
        ((2, rows, TILE), BF16),
        ((rows, TILE), BF16),
        ((rows, TILE), BF16),
        ((2 * kids, TILE), BF16),
        ((2 * kids, TILE), BF16),
    ]
    dma = pltpu.SemaphoreType.DMA
    return pl.pallas_call(
        functools.partial(kernel, wide, narrow, per_peer, mask_rows),
        out_shape=pltpu.VMEM((rows, probe_cols // narrow), BF16),
        in_specs=[pl.BlockSpec(memory_space=pltpu.HBM)] * 5,
        out_specs=pl.BlockSpec(memory_space=pltpu.VMEM),
        scratch_shapes=[pltpu.VMEM(shape, dtype) for shape, dtype in shapes]
        + [dma((8,)), dma((4,)), dma((6,)), dma((2,)), dma((2,)), dma((2,)), pltpu.SemaphoreType.REGULAR],
        compiler_params=pltpu.CompilerParams(
            collective_id=0, has_side_effects=True,
            vmem_limit_bytes=56 * 1024 * 1024,
        ),
    )(parent_front, child_updates, child_map.reshape(1, -1), tile_mask, probes)


def solution(mesh):
    placed = (
        P("wide", "narrow"),
        P("wide", "narrow"),
        P("wide"),
        P("wide", "narrow"),
        P("narrow", None),
    )
    return jax.shard_map(
        functools.partial(local, mesh.shape["wide"], mesh.shape["narrow"]),
        mesh=mesh, in_specs=placed, out_specs=P("wide", "narrow"), check_vma=False,
    )
```

```python
import functools

import jax
import jax.numpy as jnp
from jax import lax
from jax.experimental import pallas as pl
from jax.experimental.pallas import tpu as pltpu
from jax.sharding import PartitionSpec as P

TILE = 128
GROUP = 8
MESH = pl.DeviceIdType.MESH
F32 = jnp.float32
BF16 = jnp.bfloat16


def repeat(count, body):
    if count == 1:
        body(0)
    else:
        lax.fori_loop(0, count, lambda i, carry: (body(i), carry)[1], 0)


def iota(shape, dim):
    return lax.broadcasted_iota(jnp.int32, shape, dim)


def kernel(
    wide, narrow, per_peer, mask_rows,
    parent_in, child_in, map_in, mask_in, probes_in,
    out_ref,
    parent, child, cmap, mask, probes, mask_pad,
    probes_far, msg_out, msg_in, mask_far, pick, sorted_rows, lands,
    f_own, f_core, f_send, f_x,
    z_out, z_in,
    load_sem, msg_sem, far_sem, z_sem, pair_send, pair_recv, ready,
):
    rows, cols = parent.shape
    _, kids, touched = child.shape
    slots = GROUP * per_peer
    groups = wide // GROUP
    row_tile = rows // mask.shape[0]
    me_w = lax.axis_index("wide")
    me_n = lax.axis_index("narrow")
    core = lax.rem(me_n, 2)
    along = lax.div(me_n, 2)
    core_narrow = me_n + 1 - 2 * core
    core_peer = (me_w, core_narrow)
    x_narrow = lax.rem(me_n + 2, narrow)
    x_peer = (me_w, x_narrow)

    def each_peer(fn, first=1):
        def one(k):
            fn(lax.rem(me_w + k, wide))

        if wide <= GROUP:
            for k in range(first, wide):
                one(k)
        else:
            lax.fori_loop(first, wide, lambda k, carry: (one(k), carry)[1], 0)

    def block_at(index, size):
        return pl.ds(pl.multiple_of(index * size, size), size)

    barrier = pltpu.get_barrier_semaphore()

    def greet(device):
        pl.semaphore_signal(barrier, inc=1, device_id=device, device_id_type=MESH)

    pairs = [(map_in, cmap), (mask_in, mask), (child_in, child.at[0]), (parent_in, parent)]
    for n in range(narrow):
        pairs.append(
            (
                probes_in.at[:, n * TILE : (n + 1) * TILE],
                probes.at[n % 2, :, n // 2 * TILE : (n // 2 + 1) * TILE],
            )
        )
    loads = [
        pltpu.make_async_copy(src, dst, load_sem.at[i]) for i, (src, dst) in enumerate(pairs)
    ]
    for load in loads[:2]:
        load.start()
    each_peer(lambda w: greet((w, me_n)))
    each_peer(lambda w: greet((w, core_narrow)), first=0)
    greet(x_peer)
    for load in loads[2:]:
        load.start()

    def remote(src, dst, send, recv, device):
        return pltpu.make_async_remote_copy(
            src_ref=src, dst_ref=dst, send_sem=send, recv_sem=recv,
            device_id=device, device_id_type=MESH,
        )

    loads[0].wait()
    child_rows = cmap[...]

    def order_group(g):
        first = g * GROUP
        low = (iota((2 * GROUP, 1), 0) + first) * rows
        chosen = (child_rows >= low) & (child_rows < low + rows)
        ones = jnp.where(chosen, 1.0, 0.0)
        before = []
        step = min(kids, 256)
        for start in range(0, kids, step):
            upper = iota((kids, step), 0) < iota((kids, step), 1) + start
            before.append(
                jnp.dot(
                    ones.astype(BF16),
                    jnp.where(upper, 1.0, 0.0).astype(BF16),
                    preferred_element_type=F32,
                )
            )
        rank = before[0] if len(before) == 1 else jnp.concatenate(before, axis=1)
        rank = jnp.where(chosen, rank, -1.0)
        wanted = iota((per_peer, kids), 0).astype(F32)
        base = jnp.zeros((1, kids), jnp.int32)
        for w in range(GROUP):
            here = rank[w : w + 1, :]
            pick[block_at(first + w, per_peer), :] = jnp.where(here == wanted, 1.0, 0.0).astype(BF16)
            base = jnp.where(here >= 0.0, (first + w) * rows, base)
        local = child_rows - base
        high = (local >> 4).astype(F32)
        less = (local & 15).astype(F32)
        line = iota((TILE, kids), 0)
        coded = jnp.where(line == 0, high, jnp.where(line == 1, less, 0.0)).astype(BF16)
        places = lax.dot_general(
            pick[block_at(g, slots), :], coded, (((1,), (1,)), ((), ())), preferred_element_type=F32
        ).astype(BF16)
        msg_out[pl.ds(first, GROUP), :per_peer, :] = places.reshape(GROUP, per_peer, TILE)

    def sort_group(g, source):
        sorted_rows[block_at(g, slots), source * touched : (source + 1) * touched] = jnp.dot(
            pick[block_at(g, slots), :], child[source], preferred_element_type=F32
        ).astype(BF16)

    repeat(groups, order_group)

    loads[1].wait()
    mask_pad[...] = jnp.zeros(mask_pad.shape, BF16)
    mask_pad[: mask.shape[0], : mask.shape[1]] = mask[...].astype(F32).astype(BF16)
    my_mask = mask_pad[...]
    repeat(groups, lambda g: msg_out.__setitem__(
        (pl.ds(g * GROUP, GROUP), slice(per_peer, per_peer + mask_rows)),
        jnp.broadcast_to(my_mask[None], (GROUP, mask_rows, TILE)),
    ))

    loads[2].wait()
    repeat(groups, lambda g: sort_group(g, 0))

    part = 384 if rows % 384 == 0 else rows

    def parent_mask(i):
        at = iota((part, mask_rows), 0) + i * part
        tile = iota((part, mask_rows), 1) * row_tile
        spread = jnp.where((at >= tile) & (at < tile + row_tile), 1.0, 0.0).astype(BF16)
        kept = jnp.dot(spread, my_mask, preferred_element_type=F32).astype(BF16)
        here = block_at(i, part)
        for t in range(cols // TILE):
            span = slice(t * TILE, (t + 1) * TILE)
            parent[here, span] = parent[here, span] * kept[:, t : t + 1]

    def parent_half(half):
        def one(i):
            product = jnp.dot(
                parent[block_at(i, part), :], probes[half], preferred_element_type=F32
            ).astype(BF16)
            for x in range(2):
                f_own[half, x, block_at(i, part), :] = product[:, x * TILE : (x + 1) * TILE]

        repeat(rows // part, one)

    loads[3].wait()
    repeat(rows // part, parent_mask)
    for load in loads[4:]:
        load.wait()
    parent_half(1 - core)

    pl.semaphore_wait(barrier, 2 * wide)

    far_copies = [remote(child_in, child.at[1], far_sem.at[0], far_sem.at[1], core_peer)]
    for x in range(2):
        span = pl.ds(pl.multiple_of((2 * x + 1 - core) * TILE, TILE), TILE)
        far_copies.append(
            remote(
                probes_in.at[:touched, span], probes_far.at[:, x * TILE : (x + 1) * TILE],
                far_sem.at[2 + 2 * x], far_sem.at[3 + 2 * x], core_peer,
            )
        )

    each_peer(
        lambda w: remote(
            msg_out.at[w], msg_in.at[me_w], msg_sem.at[0], msg_sem.at[1], (w, me_n)
        ).start()
    )
    for copy in far_copies:
        copy.start()
    each_peer(
        lambda w: remote(
            mask_pad, mask_far.at[me_w], msg_sem.at[2], msg_sem.at[3], (w, core_narrow)
        ).start(),
        first=0,
    )
    msg_in[me_w] = msg_out[me_w]
    masks = remote(mask_far, mask_far, msg_sem.at[2], msg_sem.at[3], core_peer)
    messages = remote(
        msg_out.at[pl.ds(0, wide - 1)], msg_in.at[pl.ds(0, wide - 1)],
        msg_sem.at[0], msg_sem.at[1], x_peer,
    )

    f_pair = remote(f_own.at[1 - core], f_core, pair_send.at[0], pair_recv.at[0], core_peer)
    f_pair.start()
    parent_half(core)
    far_copies[0].wait_recv()
    repeat(groups, lambda g: sort_group(g, 1))

    shift = mask_rows.bit_length() - 1

    def landing(g):
        place = msg_out[pl.ds(g * GROUP, GROUP), :per_peer, :].reshape(slots, TILE).astype(F32)
        place = place[:, 0:1] * 16.0 + place[:, 1:2]
        lane = iota((slots, GROUP * mask_rows), 1)
        peer = iota((slots, GROUP * mask_rows), 0) >> (per_peer.bit_length() - 1)
        tile = ((lane & (mask_rows - 1)) * row_tile).astype(F32)
        same = ((lane >> shift) == peer) & (place >= tile) & (place < tile + row_tile)
        return jnp.where(same, 1.0, 0.0).astype(BF16)

    def child_mask(g, tiles):
        table = msg_in[pl.ds(g * GROUP, GROUP), per_peer:, :].reshape(GROUP * mask_rows, TILE)
        far = mask_far[pl.ds(g * GROUP, GROUP)].reshape(GROUP * mask_rows, TILE)
        here = block_at(g, slots)
        count = touched // TILE
        for source, part_table in enumerate((table, far)):
            kept = jnp.dot(tiles, part_table, preferred_element_type=F32).astype(BF16)
            for t in range(count):
                span = slice((source * count + t) * TILE, (source * count + t + 1) * TILE)
                sorted_rows[here, span] = sorted_rows[here, span] * kept[:, t : t + 1]

    def child_product(g):
        here = block_at(g, slots)
        product = jnp.dot(
            sorted_rows[here, :touched], probes[core, :touched, :], preferred_element_type=F32
        ) + jnp.dot(sorted_rows[here, touched:], probes_far[...], preferred_element_type=F32)
        product = product.astype(BF16)
        for x in range(2):
            z_out[block_at(x * groups + g, slots), :] = product[:, x * TILE : (x + 1) * TILE]

    f_pair.wait_recv()
    f_send[...] = (f_own[core, 1 - along].astype(F32) + f_core[1 - along].astype(F32)).astype(BF16)
    f_cross = remote(f_send, f_x, pair_send.at[1], pair_recv.at[1], x_peer)
    f_cross.start()

    def all_in():
        messages.wait_recv()
        pl.semaphore_signal(ready, inc=1, device_id=x_peer, device_id_type=MESH)
        masks.wait_recv()

    if groups == 1:
        tiles = landing(0)
        all_in()
        child_mask(0, tiles)
    else:
        all_in()
        repeat(groups, lambda g: child_mask(g, landing(g)))
    for copy in far_copies[1:]:
        copy.wait_recv()
    repeat(groups, child_product)

    def z_start(x, n, w):
        remote(
            z_out.at[block_at(x * wide + w, per_peer)],
            z_in.at[block_at(along * wide + me_w, per_peer)],
            z_sem.at[0], z_sem.at[1], (w, n),
        ).start()

    pl.semaphore_wait(ready, 1)
    each_peer(lambda w: z_start(1 - along, x_narrow, w), first=0)
    each_peer(lambda w: z_start(along, me_n, w))
    mine = block_at(along * wide + me_w, per_peer)
    z_in[mine, :] = z_out[mine, :]
    most = pl.ds(0, (2 * wide - 1) * per_peer)
    arrivals = remote(z_out.at[most], z_in.at[most], z_sem.at[0], z_sem.at[1], x_peer)

    for g in range(groups):
        place = msg_in[g * GROUP : (g + 1) * GROUP, :per_peer, :].reshape(slots, TILE)
        lane = iota((2 * GROUP, TILE), 1)
        weigh = jnp.where(lane == 0, 16.0, jnp.where(lane == 1, 1.0, 0.0)).astype(BF16)
        place = lax.dot_general(
            weigh, place, (((1,), (1,)), ((), ())), preferred_element_type=F32
        )[0:1, :]
        lands[:, g * slots : (g + 1) * slots] = jnp.where(
            place == iota((rows, slots), 0).astype(F32), 1.0, 0.0
        ).astype(BF16)
    f_cross.wait_recv()
    total = f_own[core, along].astype(F32) + f_core[along].astype(F32) + f_x[...].astype(F32)
    arrivals.wait_recv()
    both_chips = jnp.concatenate([z_in[:kids, :], z_in[kids:, :]], axis=1)
    added = jnp.dot(lands[...], both_chips, preferred_element_type=F32)
    out_ref[...] = (total + (added[:, :TILE] + added[:, TILE:])).astype(out_ref.dtype)

    messages.wait_send()
    masks.wait_send()
    arrivals.wait_send()
    for copy in (f_pair, f_cross, *far_copies):
        copy.wait_send()


def local(wide, narrow, parent_front, child_updates, child_map, tile_mask, probes):
    rows, cols = parent_front.shape
    kids, touched = child_updates.shape
    per_peer = kids // wide
    probe_cols = probes.shape[1]
    mask_rows = 16 * pl.cdiv(tile_mask.shape[0], 16)
    shapes = [
        ((rows, cols), BF16),
        ((2, kids, touched), BF16),
        ((1, kids), jnp.int32),
        (tile_mask.shape, jnp.int32),
        ((2, cols, 2 * TILE), BF16),
        ((mask_rows, TILE), BF16),
        ((touched, 2 * TILE), BF16),
        ((wide, per_peer + mask_rows, TILE), BF16),
        ((wide, per_peer + mask_rows, TILE), BF16),
        ((wide, mask_rows, TILE), BF16),
        ((kids, kids), BF16),
        ((kids, 2 * touched), BF16),
        ((rows, kids), BF16),
        ((2, 2, rows, TILE), BF16),
        ((2, rows, TILE), BF16),
        ((rows, TILE), BF16),
        ((rows, TILE), BF16),
        ((2 * kids, TILE), BF16),
        ((2 * kids, TILE), BF16),
    ]
    dma = pltpu.SemaphoreType.DMA
    return pl.pallas_call(
        functools.partial(kernel, wide, narrow, per_peer, mask_rows),
        out_shape=pltpu.VMEM((rows, probe_cols // narrow), BF16),
        in_specs=[pl.BlockSpec(memory_space=pltpu.HBM)] * 5,
        out_specs=pl.BlockSpec(memory_space=pltpu.VMEM),
        scratch_shapes=[pltpu.VMEM(shape, dtype) for shape, dtype in shapes]
        + [dma((8,)), dma((4,)), dma((6,)), dma((2,)), dma((2,)), dma((2,)), pltpu.SemaphoreType.REGULAR],
        compiler_params=pltpu.CompilerParams(
            collective_id=0, has_side_effects=True,
            vmem_limit_bytes=56 * 1024 * 1024,
        ),
    )(parent_front, child_updates, child_map.reshape(1, -1), tile_mask, probes)


def solution(mesh):
    placed = (
        P("wide", "narrow"),
        P("wide", "narrow"),
        P("wide"),
        P("wide", "narrow"),
        P("narrow", None),
    )
    return jax.shard_map(
        functools.partial(local, mesh.shape["wide"], mesh.shape["narrow"]),
        mesh=mesh, in_specs=placed, out_specs=P("wide", "narrow"), check_vma=False,
    )
```

```python
import functools

import jax
import jax.numpy as jnp
from jax import lax
from jax.experimental import pallas as pl
from jax.experimental.pallas import tpu as pltpu
from jax.sharding import PartitionSpec as P

TILE = 128
GROUP = 8
MESH = pl.DeviceIdType.MESH
F32 = jnp.float32
BF16 = jnp.bfloat16


def repeat(count, body):
    if count == 1:
        body(0)
    else:
        lax.fori_loop(0, count, lambda i, carry: (body(i), carry)[1], 0)


def iota(shape, dim):
    return lax.broadcasted_iota(jnp.int32, shape, dim)


def kernel(
    wide, narrow, per_peer, mask_rows,
    parent_in, child_in, map_in, mask_in, probes_in,
    out_ref,
    parent, child, cmap, mask, probes, mask_pad,
    probes_far, msg_out, msg_in, mask_far, pick, sorted_rows, lands,
    f_own, f_core, f_send, f_x,
    z_out, z_in,
    load_sem, msg_sem, far_sem, z_sem, pair_send, pair_recv, ready,
):
    rows, cols = parent.shape
    _, kids, touched = child.shape
    slots = GROUP * per_peer
    groups = wide // GROUP
    row_tile = rows // mask.shape[0]
    me_w = lax.axis_index("wide")
    me_n = lax.axis_index("narrow")
    core = lax.rem(me_n, 2)
    along = lax.div(me_n, 2)
    core_narrow = me_n + 1 - 2 * core
    core_peer = (me_w, core_narrow)
    x_narrow = lax.rem(me_n + 2, narrow)
    x_peer = (me_w, x_narrow)

    half_wide = wide // 2
    my_half = lax.div(me_w, half_wide)
    my_place = lax.rem(me_w, half_wide)

    def run(first, one):
        if wide <= GROUP:
            for k in range(first, half_wide):
                one(k)
        else:
            lax.fori_loop(first, half_wide, lambda k, carry: (one(k), carry)[1], 0)

    def each_far(fn):
        def one(k):
            place = lax.rem(2 * half_wide - 1 - my_place + k, half_wide)
            fn((1 - my_half) * half_wide + place)

        run(0, one)

    def each_near(fn, first=1):
        def one(k):
            fn(my_half * half_wide + lax.rem(my_place + k, half_wide))

        run(first, one)

    def each_peer(fn):
        each_far(fn)
        each_near(fn)

    def block_at(index, size):
        return pl.ds(pl.multiple_of(index * size, size), size)

    barrier = pltpu.get_barrier_semaphore()

    def greet(device):
        pl.semaphore_signal(barrier, inc=1, device_id=device, device_id_type=MESH)

    pairs = [(map_in, cmap), (mask_in, mask), (child_in, child.at[0]), (parent_in, parent)]
    for n in range(narrow):
        pairs.append(
            (
                probes_in.at[:, n * TILE : (n + 1) * TILE],
                probes.at[n % 2, :, n // 2 * TILE : (n // 2 + 1) * TILE],
            )
        )
    loads = [
        pltpu.make_async_copy(src, dst, load_sem.at[i]) for i, (src, dst) in enumerate(pairs)
    ]
    for load in loads[:2]:
        load.start()
    def greet_both(w):
        greet((w, me_n))
        greet((w, core_narrow))

    each_peer(greet_both)
    greet(core_peer)
    greet(x_peer)
    for load in loads[2:]:
        load.start()

    def remote(src, dst, send, recv, device):
        return pltpu.make_async_remote_copy(
            src_ref=src, dst_ref=dst, send_sem=send, recv_sem=recv,
            device_id=device, device_id_type=MESH,
        )

    loads[0].wait()
    child_rows = cmap[...]

    def order_group(g):
        first = g * GROUP
        low = (iota((2 * GROUP, 1), 0) + first) * rows
        chosen = (child_rows >= low) & (child_rows < low + rows)
        ones = jnp.where(chosen, 1.0, 0.0)
        before = []
        step = min(kids, 256)
        for start in range(0, kids, step):
            upper = iota((kids, step), 0) < iota((kids, step), 1) + start
            before.append(
                jnp.dot(
                    ones.astype(BF16),
                    jnp.where(upper, 1.0, 0.0).astype(BF16),
                    preferred_element_type=F32,
                )
            )
        rank = before[0] if len(before) == 1 else jnp.concatenate(before, axis=1)
        rank = jnp.where(chosen, rank, -1.0)
        wanted = iota((per_peer, kids), 0).astype(F32)
        base = jnp.zeros((1, kids), jnp.int32)
        for w in range(GROUP):
            here = rank[w : w + 1, :]
            pick[block_at(first + w, per_peer), :] = jnp.where(here == wanted, 1.0, 0.0).astype(BF16)
            base = jnp.where(here >= 0.0, (first + w) * rows, base)
        local = child_rows - base
        high = (local >> 4).astype(F32)
        less = (local & 15).astype(F32)
        line = iota((TILE, kids), 0)
        coded = jnp.where(line == 0, high, jnp.where(line == 1, less, 0.0)).astype(BF16)
        places = lax.dot_general(
            pick[block_at(g, slots), :], coded, (((1,), (1,)), ((), ())), preferred_element_type=F32
        ).astype(BF16)
        msg_out[pl.ds(first, GROUP), :per_peer, :] = places.reshape(GROUP, per_peer, TILE)

    def sort_group(g, source):
        sorted_rows[block_at(g, slots), source * touched : (source + 1) * touched] = jnp.dot(
            pick[block_at(g, slots), :], child[source], preferred_element_type=F32
        ).astype(BF16)

    repeat(groups, order_group)

    loads[1].wait()
    mask_pad[...] = jnp.zeros(mask_pad.shape, BF16)
    mask_pad[: mask.shape[0], : mask.shape[1]] = mask[...].astype(F32).astype(BF16)
    my_mask = mask_pad[...]
    repeat(groups, lambda g: msg_out.__setitem__(
        (pl.ds(g * GROUP, GROUP), slice(per_peer, per_peer + mask_rows)),
        jnp.broadcast_to(my_mask[None], (GROUP, mask_rows, TILE)),
    ))

    loads[2].wait()
    repeat(groups, lambda g: sort_group(g, 0))

    part = 384 if rows % 384 == 0 else rows

    def parent_mask(i):
        at = iota((part, mask_rows), 0) + i * part
        tile = iota((part, mask_rows), 1) * row_tile
        spread = jnp.where((at >= tile) & (at < tile + row_tile), 1.0, 0.0).astype(BF16)
        kept = jnp.dot(spread, my_mask, preferred_element_type=F32).astype(BF16)
        here = block_at(i, part)
        for t in range(cols // TILE):
            span = slice(t * TILE, (t + 1) * TILE)
            parent[here, span] = parent[here, span] * kept[:, t : t + 1]

    def parent_half(half):
        def one(i):
            product = jnp.dot(
                parent[block_at(i, part), :], probes[half], preferred_element_type=F32
            ).astype(BF16)
            for x in range(2):
                f_own[half, x, block_at(i, part), :] = product[:, x * TILE : (x + 1) * TILE]

        repeat(rows // part, one)

    loads[3].wait()
    repeat(rows // part, parent_mask)
    for load in loads[4:]:
        load.wait()
    parent_half(1 - core)

    pl.semaphore_wait(barrier, 2 * wide)
    pl.semaphore_signal(ready, inc=1, device_id=x_peer, device_id_type=MESH)

    far_copies = [remote(child_in, child.at[1], far_sem.at[0], far_sem.at[1], core_peer)]
    for x in range(2):
        span = pl.ds(pl.multiple_of((2 * x + 1 - core) * TILE, TILE), TILE)
        far_copies.append(
            remote(
                probes_in.at[:touched, span], probes_far.at[:, x * TILE : (x + 1) * TILE],
                far_sem.at[2 + 2 * x], far_sem.at[3 + 2 * x], core_peer,
            )
        )

    def tell_mask(w):
        remote(mask_pad, mask_far.at[me_w], msg_sem.at[2], msg_sem.at[3], (w, core_narrow)).start()

    def tell(w):
        remote(msg_out.at[w], msg_in.at[me_w], msg_sem.at[0], msg_sem.at[1], (w, me_n)).start()
        tell_mask(w)

    each_peer(tell)
    tell_mask(me_w)
    for copy in far_copies:
        copy.start()
    msg_in[me_w] = msg_out[me_w]
    masks = remote(mask_far, mask_far, msg_sem.at[2], msg_sem.at[3], core_peer)
    messages = remote(
        msg_out.at[pl.ds(0, wide - 1)], msg_in.at[pl.ds(0, wide - 1)],
        msg_sem.at[0], msg_sem.at[1], x_peer,
    )

    f_pair = remote(f_own.at[1 - core], f_core, pair_send.at[0], pair_recv.at[0], core_peer)
    f_pair.start()
    parent_half(core)
    far_copies[0].wait_recv()
    repeat(groups, lambda g: sort_group(g, 1))

    shift = mask_rows.bit_length() - 1

    def landing(g):
        place = msg_out[pl.ds(g * GROUP, GROUP), :per_peer, :].reshape(slots, TILE).astype(F32)
        place = place[:, 0:1] * 16.0 + place[:, 1:2]
        lane = iota((slots, GROUP * mask_rows), 1)
        peer = iota((slots, GROUP * mask_rows), 0) >> (per_peer.bit_length() - 1)
        tile = ((lane & (mask_rows - 1)) * row_tile).astype(F32)
        same = ((lane >> shift) == peer) & (place >= tile) & (place < tile + row_tile)
        return jnp.where(same, 1.0, 0.0).astype(BF16)

    def child_mask(g, tiles):
        table = msg_in[pl.ds(g * GROUP, GROUP), per_peer:, :].reshape(GROUP * mask_rows, TILE)
        far = mask_far[pl.ds(g * GROUP, GROUP)].reshape(GROUP * mask_rows, TILE)
        here = block_at(g, slots)
        count = touched // TILE
        for source, part_table in enumerate((table, far)):
            kept = jnp.dot(tiles, part_table, preferred_element_type=F32).astype(BF16)
            for t in range(count):
                span = slice((source * count + t) * TILE, (source * count + t + 1) * TILE)
                sorted_rows[here, span] = sorted_rows[here, span] * kept[:, t : t + 1]

    def child_product(g):
        here = block_at(g, slots)
        product = jnp.dot(
            sorted_rows[here, :touched], probes[core, :touched, :], preferred_element_type=F32
        ) + jnp.dot(sorted_rows[here, touched:], probes_far[...], preferred_element_type=F32)
        product = product.astype(BF16)
        for x in range(2):
            z_out[block_at(x * groups + g, slots), :] = product[:, x * TILE : (x + 1) * TILE]

    f_pair.wait_recv()
    f_send[...] = (f_own[core, 1 - along].astype(F32) + f_core[1 - along].astype(F32)).astype(BF16)
    f_cross = remote(f_send, f_x, pair_send.at[1], pair_recv.at[1], x_peer)
    f_cross.start()

    def all_in():
        messages.wait_recv()
        masks.wait_recv()

    if groups == 1:
        tiles = landing(0)
        all_in()
        child_mask(0, tiles)
    else:
        all_in()
        repeat(groups, lambda g: child_mask(g, landing(g)))
    for copy in far_copies[1:]:
        copy.wait_recv()
    repeat(groups, child_product)

    def z_start(x, n, w):
        remote(
            z_out.at[block_at(x * wide + w, per_peer)],
            z_in.at[block_at(along * wide + me_w, per_peer)],
            z_sem.at[0], z_sem.at[1], (w, n),
        ).start()

    pl.semaphore_wait(ready, 1)
    def z_both(w):
        z_start(1 - along, x_narrow, w)
        z_start(along, me_n, w)

    each_peer(z_both)
    z_start(1 - along, x_narrow, me_w)
    mine = block_at(along * wide + me_w, per_peer)
    z_in[mine, :] = z_out[mine, :]
    most = pl.ds(0, (2 * wide - 1) * per_peer)
    arrivals = remote(z_out.at[most], z_in.at[most], z_sem.at[0], z_sem.at[1], x_peer)

    for g in range(groups):
        place = msg_in[g * GROUP : (g + 1) * GROUP, :per_peer, :].reshape(slots, TILE)
        lane = iota((2 * GROUP, TILE), 1)
        weigh = jnp.where(lane == 0, 16.0, jnp.where(lane == 1, 1.0, 0.0)).astype(BF16)
        place = lax.dot_general(
            weigh, place, (((1,), (1,)), ((), ())), preferred_element_type=F32
        )[0:1, :]
        lands[:, g * slots : (g + 1) * slots] = jnp.where(
            place == iota((rows, slots), 0).astype(F32), 1.0, 0.0
        ).astype(BF16)
    f_cross.wait_recv()
    total = f_own[core, along].astype(F32) + f_core[along].astype(F32) + f_x[...].astype(F32)
    arrivals.wait_recv()
    both_chips = jnp.concatenate([z_in[:kids, :], z_in[kids:, :]], axis=1)
    added = jnp.dot(lands[...], both_chips, preferred_element_type=F32)
    out_ref[...] = (total + (added[:, :TILE] + added[:, TILE:])).astype(out_ref.dtype)

    messages.wait_send()
    masks.wait_send()
    arrivals.wait_send()
    for copy in (f_pair, f_cross, *far_copies):
        copy.wait_send()


def local(wide, narrow, parent_front, child_updates, child_map, tile_mask, probes):
    rows, cols = parent_front.shape
    kids, touched = child_updates.shape
    per_peer = kids // wide
    probe_cols = probes.shape[1]
    mask_rows = 16 * pl.cdiv(tile_mask.shape[0], 16)
    shapes = [
        ((rows, cols), BF16),
        ((2, kids, touched), BF16),
        ((1, kids), jnp.int32),
        (tile_mask.shape, jnp.int32),
        ((2, cols, 2 * TILE), BF16),
        ((mask_rows, TILE), BF16),
        ((touched, 2 * TILE), BF16),
        ((wide, per_peer + mask_rows, TILE), BF16),
        ((wide, per_peer + mask_rows, TILE), BF16),
        ((wide, mask_rows, TILE), BF16),
        ((kids, kids), BF16),
        ((kids, 2 * touched), BF16),
        ((rows, kids), BF16),
        ((2, 2, rows, TILE), BF16),
        ((2, rows, TILE), BF16),
        ((rows, TILE), BF16),
        ((rows, TILE), BF16),
        ((2 * kids, TILE), BF16),
        ((2 * kids, TILE), BF16),
    ]
    dma = pltpu.SemaphoreType.DMA
    return pl.pallas_call(
        functools.partial(kernel, wide, narrow, per_peer, mask_rows),
        out_shape=pltpu.VMEM((rows, probe_cols // narrow), BF16),
        in_specs=[pl.BlockSpec(memory_space=pltpu.HBM)] * 5,
        out_specs=pl.BlockSpec(memory_space=pltpu.VMEM),
        scratch_shapes=[pltpu.VMEM(shape, dtype) for shape, dtype in shapes]
        + [dma((8,)), dma((4,)), dma((6,)), dma((2,)), dma((2,)), dma((2,)), pltpu.SemaphoreType.REGULAR],
        compiler_params=pltpu.CompilerParams(
            collective_id=0, has_side_effects=True,
            vmem_limit_bytes=56 * 1024 * 1024,
        ),
    )(parent_front, child_updates, child_map.reshape(1, -1), tile_mask, probes)


def solution(mesh):
    placed = (
        P("wide", "narrow"),
        P("wide", "narrow"),
        P("wide"),
        P("wide", "narrow"),
        P("narrow", None),
    )
    return jax.shard_map(
        functools.partial(local, mesh.shape["wide"], mesh.shape["narrow"]),
        mesh=mesh, in_specs=placed, out_specs=P("wide", "narrow"), check_vma=False,
    )
```

```python
import functools

import jax
import jax.numpy as jnp
from jax import lax
from jax.experimental import pallas as pl
from jax.experimental.pallas import tpu as pltpu
from jax.sharding import PartitionSpec as P

TILE = 128
GROUP = 8
MESH = pl.DeviceIdType.MESH
F32 = jnp.float32
BF16 = jnp.bfloat16


def repeat(count, body):
    if count == 1:
        body(0)
    else:
        lax.fori_loop(0, count, lambda i, carry: (body(i), carry)[1], 0)


def iota(shape, dim):
    return lax.broadcasted_iota(jnp.int32, shape, dim)


def kernel(
    wide, narrow, per_peer, mask_rows,
    parent_in, child_in, map_in, mask_in, probes_in,
    out_ref,
    parent, child, cmap, mask, probes, mask_pad,
    probes_far, msg_out, msg_in, mask_far, pick, sorted_rows, lands,
    f_own, f_core, f_send, f_x,
    z_out, z_in,
    load_sem, msg_sem, far_sem, z_sem, pair_send, pair_recv, ready,
):
    rows, cols = parent.shape
    _, kids, touched = child.shape
    slots = GROUP * per_peer
    groups = wide // GROUP
    row_tile = rows // mask.shape[0]
    me_w = lax.axis_index("wide")
    me_n = lax.axis_index("narrow")
    core = lax.rem(me_n, 2)
    along = lax.div(me_n, 2)
    core_narrow = me_n + 1 - 2 * core
    core_peer = (me_w, core_narrow)
    x_narrow = lax.rem(me_n + 2, narrow)
    x_peer = (me_w, x_narrow)

    half_wide = wide // 2
    my_half = lax.div(me_w, half_wide)
    my_place = lax.rem(me_w, half_wide)

    def run(first, one):
        if wide <= GROUP:
            for k in range(first, half_wide):
                one(k)
        else:
            lax.fori_loop(first, half_wide, lambda k, carry: (one(k), carry)[1], 0)

    def each_far(fn):
        def one(k):
            place = lax.rem(2 * half_wide - 1 - my_place + k, half_wide)
            fn((1 - my_half) * half_wide + place)

        run(0, one)

    def each_near(fn, first=1):
        def one(k):
            fn(my_half * half_wide + lax.rem(my_place + k, half_wide))

        run(first, one)

    def each_peer(fn):
        each_far(fn)
        each_near(fn)

    def block_at(index, size):
        return pl.ds(pl.multiple_of(index * size, size), size)

    barrier = pltpu.get_barrier_semaphore()

    def greet(device):
        pl.semaphore_signal(barrier, inc=1, device_id=device, device_id_type=MESH)

    pairs = [(map_in, cmap), (mask_in, mask), (child_in, child.at[0]), (parent_in, parent)]
    for n in range(narrow):
        pairs.append(
            (
                probes_in.at[:, n * TILE : (n + 1) * TILE],
                probes.at[n % 2, :, n // 2 * TILE : (n // 2 + 1) * TILE],
            )
        )
    loads = [
        pltpu.make_async_copy(src, dst, load_sem.at[i]) for i, (src, dst) in enumerate(pairs)
    ]
    for load in loads[:2]:
        load.start()
    def greet_both(w):
        greet((w, me_n))
        greet((w, core_narrow))

    each_peer(greet_both)
    greet(core_peer)
    greet(x_peer)
    for load in loads[2:]:
        load.start()

    def remote(src, dst, send, recv, device):
        return pltpu.make_async_remote_copy(
            src_ref=src, dst_ref=dst, send_sem=send, recv_sem=recv,
            device_id=device, device_id_type=MESH,
        )

    loads[0].wait()
    child_rows = cmap[...]

    def order_group(g):
        first = g * GROUP
        low = (iota((2 * GROUP, 1), 0) + first) * rows
        chosen = (child_rows >= low) & (child_rows < low + rows)
        ones = jnp.where(chosen, 1.0, 0.0)
        before = []
        step = min(kids, 256)
        for start in range(0, kids, step):
            upper = iota((kids, step), 0) < iota((kids, step), 1) + start
            before.append(
                jnp.dot(
                    ones.astype(BF16),
                    jnp.where(upper, 1.0, 0.0).astype(BF16),
                    preferred_element_type=F32,
                )
            )
        rank = before[0] if len(before) == 1 else jnp.concatenate(before, axis=1)
        rank = jnp.where(chosen, rank, -1.0)
        wanted = iota((per_peer, kids), 0).astype(F32)
        base = jnp.zeros((1, kids), jnp.int32)
        for w in range(GROUP):
            here = rank[w : w + 1, :]
            pick[block_at(first + w, per_peer), :] = jnp.where(here == wanted, 1.0, 0.0).astype(BF16)
            base = jnp.where(here >= 0.0, (first + w) * rows, base)
        local = child_rows - base
        high = (local >> 4).astype(F32)
        less = (local & 15).astype(F32)
        line = iota((TILE, kids), 0)
        coded = jnp.where(line == 0, high, jnp.where(line == 1, less, 0.0)).astype(BF16)
        places = lax.dot_general(
            pick[block_at(g, slots), :], coded, (((1,), (1,)), ((), ())), preferred_element_type=F32
        ).astype(BF16)
        msg_out[pl.ds(first, GROUP), :per_peer, :] = places.reshape(GROUP, per_peer, TILE)

    def sort_group(g, source):
        sorted_rows[block_at(g, slots), source * touched : (source + 1) * touched] = jnp.dot(
            pick[block_at(g, slots), :], child[source], preferred_element_type=F32
        ).astype(BF16)

    repeat(groups, order_group)

    loads[1].wait()
    mask_pad[...] = jnp.zeros(mask_pad.shape, BF16)
    mask_pad[: mask.shape[0], : mask.shape[1]] = mask[...].astype(F32).astype(BF16)
    my_mask = mask_pad[...]
    repeat(groups, lambda g: msg_out.__setitem__(
        (pl.ds(g * GROUP, GROUP), slice(per_peer, per_peer + mask_rows)),
        jnp.broadcast_to(my_mask[None], (GROUP, mask_rows, TILE)),
    ))

    loads[2].wait()
    repeat(groups, lambda g: sort_group(g, 0))

    part = 384 if rows % 384 == 0 else rows

    def parent_mask(i):
        at = iota((part, mask_rows), 0) + i * part
        tile = iota((part, mask_rows), 1) * row_tile
        spread = jnp.where((at >= tile) & (at < tile + row_tile), 1.0, 0.0).astype(BF16)
        kept = jnp.dot(spread, my_mask, preferred_element_type=F32).astype(BF16)
        here = block_at(i, part)
        for t in range(cols // TILE):
            span = slice(t * TILE, (t + 1) * TILE)
            parent[here, span] = parent[here, span] * kept[:, t : t + 1]

    def parent_half(half):
        def one(i):
            product = jnp.dot(
                parent[block_at(i, part), :], probes[half], preferred_element_type=F32
            ).astype(BF16)
            for x in range(2):
                f_own[half, x, block_at(i, part), :] = product[:, x * TILE : (x + 1) * TILE]

        repeat(rows // part, one)

    loads[3].wait()
    repeat(rows // part, parent_mask)
    for load in loads[4:]:
        load.wait()
    parent_half(1 - core)

    pl.semaphore_wait(barrier, 2 * wide)
    pl.semaphore_signal(ready, inc=1, device_id=x_peer, device_id_type=MESH)

    far_copies = [remote(child_in, child.at[1], far_sem.at[0], far_sem.at[1], core_peer)]
    for x in range(2):
        span = pl.ds(pl.multiple_of((2 * x + 1 - core) * TILE, TILE), TILE)
        far_copies.append(
            remote(
                probes_in.at[:touched, span], probes_far.at[:, x * TILE : (x + 1) * TILE],
                far_sem.at[2 + 2 * x], far_sem.at[3 + 2 * x], core_peer,
            )
        )

    def tell_mask(w, far):
        remote(
            mask_pad, mask_far.at[me_w],
            msg_sem.at[4 * far + 2], msg_sem.at[4 * far + 3], (w, core_narrow),
        ).start()

    def tell(w, far):
        remote(
            msg_out.at[w], msg_in.at[me_w],
            msg_sem.at[4 * far], msg_sem.at[4 * far + 1], (w, me_n),
        ).start()
        tell_mask(w, far)

    each_far(lambda w: tell(w, 1))
    each_near(lambda w: tell(w, 0))
    tell_mask(me_w, 0)
    for copy in far_copies:
        copy.start()
    msg_in[me_w] = msg_out[me_w]

    def all_of(buffer_out, buffer_in, count, sems, at):
        return remote(
            buffer_out.at[pl.ds(0, count)], buffer_in.at[pl.ds(0, count)],
            sems.at[at], sems.at[at + 1], x_peer,
        )

    notices = [
        (
            all_of(msg_out, msg_in, half_wide - 1 + far, msg_sem, 4 * far),
            all_of(mask_far, mask_far, half_wide, msg_sem, 4 * far + 2),
        )
        for far in range(2)
    ]

    f_pair = remote(f_own.at[1 - core], f_core, pair_send.at[0], pair_recv.at[0], core_peer)
    f_pair.start()
    parent_half(core)
    far_copies[0].wait_recv()
    repeat(groups, lambda g: sort_group(g, 1))

    shift = mask_rows.bit_length() - 1

    team = GROUP // 2
    team_slots = team * per_peer
    teams = half_wide // team

    def landing(g):
        place = msg_out[pl.ds(g * team, team), :per_peer, :].reshape(team_slots, TILE).astype(F32)
        place = place[:, 0:1] * 16.0 + place[:, 1:2]
        lane = iota((team_slots, team * mask_rows), 1)
        peer = iota((team_slots, team * mask_rows), 0) >> (per_peer.bit_length() - 1)
        tile = ((lane & (mask_rows - 1)) * row_tile).astype(F32)
        same = ((lane >> shift) == peer) & (place >= tile) & (place < tile + row_tile)
        return jnp.where(same, 1.0, 0.0).astype(BF16)

    def child_mask(g, tiles):
        table = msg_in[pl.ds(g * team, team), per_peer:, :].reshape(team * mask_rows, TILE)
        far = mask_far[pl.ds(g * team, team)].reshape(team * mask_rows, TILE)
        here = block_at(g, team_slots)
        count = touched // TILE
        for source, part_table in enumerate((table, far)):
            kept = jnp.dot(tiles, part_table, preferred_element_type=F32).astype(BF16)
            for t in range(count):
                span = slice((source * count + t) * TILE, (source * count + t + 1) * TILE)
                sorted_rows[here, span] = sorted_rows[here, span] * kept[:, t : t + 1]

    def child_product(g):
        here = block_at(g, team_slots)
        product = jnp.dot(
            sorted_rows[here, :touched], probes[core, :touched, :], preferred_element_type=F32
        ) + jnp.dot(sorted_rows[here, touched:], probes_far[...], preferred_element_type=F32)
        product = product.astype(BF16)
        for x in range(2):
            z_out[block_at(x * 2 * teams + g, team_slots), :] = product[:, x * TILE : (x + 1) * TILE]

    f_pair.wait_recv()
    f_send[...] = (f_own[core, 1 - along].astype(F32) + f_core[1 - along].astype(F32)).astype(BF16)
    f_cross = remote(f_send, f_x, pair_send.at[1], pair_recv.at[1], x_peer)
    f_cross.start()

    def z_start(x, n, w, far):
        remote(
            z_out.at[block_at(x * wide + w, per_peer)],
            z_in.at[block_at(along * wide + me_w, per_peer)],
            z_sem.at[2 * far], z_sem.at[2 * far + 1], (w, n),
        ).start()

    def z_both(w, far):
        z_start(1 - along, x_narrow, w, far)
        z_start(along, me_n, w, far)

    halves = (my_half, 1 - my_half)
    ahead = [landing(half) for half in halves] if teams == 1 else None
    for far, half in enumerate(halves):
        for notice in notices[far]:
            notice.wait_recv()
        if teams == 1:
            child_mask(half, ahead[far])
        else:
            repeat(teams, lambda i: child_mask(half * teams + i, landing(half * teams + i)))
        if far == 0:
            for copy in far_copies[1:]:
                copy.wait_recv()
        repeat(teams, lambda i: child_product(half * teams + i))
        if far == 0:
            pl.semaphore_wait(ready, 1)
            each_near(lambda w: z_both(w, 0))
            z_start(1 - along, x_narrow, me_w, 0)
            mine = block_at(along * wide + me_w, per_peer)
            z_in[mine, :] = z_out[mine, :]
        else:
            each_far(lambda w: z_both(w, 1))

    arrivals = [
        all_of(z_out, z_in, (2 * half_wide - 1 + far) * per_peer, z_sem, 2 * far)
        for far in range(2)
    ]

    for g in range(groups):
        place = msg_in[g * GROUP : (g + 1) * GROUP, :per_peer, :].reshape(slots, TILE)
        lane = iota((2 * GROUP, TILE), 1)
        weigh = jnp.where(lane == 0, 16.0, jnp.where(lane == 1, 1.0, 0.0)).astype(BF16)
        place = lax.dot_general(
            weigh, place, (((1,), (1,)), ((), ())), preferred_element_type=F32
        )[0:1, :]
        lands[:, g * slots : (g + 1) * slots] = jnp.where(
            place == iota((rows, slots), 0).astype(F32), 1.0, 0.0
        ).astype(BF16)
    f_cross.wait_recv()
    total = f_own[core, along].astype(F32) + f_core[along].astype(F32) + f_x[...].astype(F32)
    for far, half in enumerate(halves):
        arrivals[far].wait_recv()
        size = kids // 2
        both_chips = jnp.concatenate(
            [z_in[block_at(half, size), :], z_in[block_at(2 + half, size), :]], axis=1
        )
        added = jnp.dot(lands[:, block_at(half, size)], both_chips, preferred_element_type=F32)
        total = total + (added[:, :TILE] + added[:, TILE:])
    out_ref[...] = total.astype(out_ref.dtype)

    for copy in (*notices[0], *notices[1], *arrivals):
        copy.wait_send()
    for copy in (f_pair, f_cross, *far_copies):
        copy.wait_send()


def local(wide, narrow, parent_front, child_updates, child_map, tile_mask, probes):
    rows, cols = parent_front.shape
    kids, touched = child_updates.shape
    per_peer = kids // wide
    probe_cols = probes.shape[1]
    mask_rows = 16 * pl.cdiv(tile_mask.shape[0], 16)
    shapes = [
        ((rows, cols), BF16),
        ((2, kids, touched), BF16),
        ((1, kids), jnp.int32),
        (tile_mask.shape, jnp.int32),
        ((2, cols, 2 * TILE), BF16),
        ((mask_rows, TILE), BF16),
        ((touched, 2 * TILE), BF16),
        ((wide, per_peer + mask_rows, TILE), BF16),
        ((wide, per_peer + mask_rows, TILE), BF16),
        ((wide, mask_rows, TILE), BF16),
        ((kids, kids), BF16),
        ((kids, 2 * touched), BF16),
        ((rows, kids), BF16),
        ((2, 2, rows, TILE), BF16),
        ((2, rows, TILE), BF16),
        ((rows, TILE), BF16),
        ((rows, TILE), BF16),
        ((2 * kids, TILE), BF16),
        ((2 * kids, TILE), BF16),
    ]
    dma = pltpu.SemaphoreType.DMA
    return pl.pallas_call(
        functools.partial(kernel, wide, narrow, per_peer, mask_rows),
        out_shape=pltpu.VMEM((rows, probe_cols // narrow), BF16),
        in_specs=[pl.BlockSpec(memory_space=pltpu.HBM)] * 5,
        out_specs=pl.BlockSpec(memory_space=pltpu.VMEM),
        scratch_shapes=[pltpu.VMEM(shape, dtype) for shape, dtype in shapes]
        + [dma((8,)), dma((8,)), dma((6,)), dma((4,)), dma((2,)), dma((2,)), pltpu.SemaphoreType.REGULAR],
        compiler_params=pltpu.CompilerParams(
            collective_id=0, has_side_effects=True,
            vmem_limit_bytes=56 * 1024 * 1024,
        ),
    )(parent_front, child_updates, child_map.reshape(1, -1), tile_mask, probes)


def solution(mesh):
    placed = (
        P("wide", "narrow"),
        P("wide", "narrow"),
        P("wide"),
        P("wide", "narrow"),
        P("narrow", None),
    )
    return jax.shard_map(
        functools.partial(local, mesh.shape["wide"], mesh.shape["narrow"]),
        mesh=mesh, in_specs=placed, out_specs=P("wide", "narrow"), check_vma=False,
    )
```

```python
import functools

import jax
import jax.numpy as jnp
from jax import lax
from jax.experimental import pallas as pl
from jax.experimental.pallas import tpu as pltpu
from jax.sharding import PartitionSpec as P

TILE = 128
GROUP = 8
MESH = pl.DeviceIdType.MESH
F32 = jnp.float32
BF16 = jnp.bfloat16


def repeat(count, body):
    if count == 1:
        body(0)
    else:
        lax.fori_loop(0, count, lambda i, carry: (body(i), carry)[1], 0)


def iota(shape, dim):
    return lax.broadcasted_iota(jnp.int32, shape, dim)


def kernel(
    wide, narrow, per_peer, mask_rows,
    parent_in, child_in, map_in, mask_in, probes_in,
    out_ref,
    parent, child, cmap, mask, probes, mask_pad,
    probes_far, msg_out, msg_in, mask_far, pick, sorted_rows, lands,
    f_own, f_core, f_send, f_x,
    z_out, z_in, tile_products, keep,
    load_sem, msg_sem, far_sem, z_sem, pair_send, pair_recv, ready,
):
    rows, cols = parent.shape
    _, kids, touched = child.shape
    slots = GROUP * per_peer
    groups = wide // GROUP
    row_tile = rows // mask.shape[0]
    me_w = lax.axis_index("wide")
    me_n = lax.axis_index("narrow")
    core = lax.rem(me_n, 2)
    along = lax.div(me_n, 2)
    core_narrow = me_n + 1 - 2 * core
    core_peer = (me_w, core_narrow)
    x_narrow = lax.rem(me_n + 2, narrow)
    x_peer = (me_w, x_narrow)

    half_wide = wide // 2
    my_half = lax.div(me_w, half_wide)
    my_place = lax.rem(me_w, half_wide)

    def run(first, one):
        if wide <= GROUP:
            for k in range(first, half_wide):
                one(k)
        else:
            lax.fori_loop(first, half_wide, lambda k, carry: (one(k), carry)[1], 0)

    def each_far(fn):
        def one(k):
            fn((1 - my_half) * (wide - 1 - k) + my_half * k)

        run(0, one)

    def each_near(fn, first=1):
        def one(k):
            fn(my_half * half_wide + lax.rem(my_place + k, half_wide))

        run(first, one)

    def each_peer(fn):
        each_far(fn)
        each_near(fn)

    def block_at(index, size):
        return pl.ds(pl.multiple_of(index * size, size), size)

    barrier = pltpu.get_barrier_semaphore()

    def greet(device):
        pl.semaphore_signal(barrier, inc=1, device_id=device, device_id_type=MESH)

    pairs = [(map_in, cmap), (mask_in, mask), (child_in, child.at[0]), (parent_in, parent)]
    for n in range(narrow):
        pairs.append(
            (
                probes_in.at[:, n * TILE : (n + 1) * TILE],
                probes.at[n % 2, :, n // 2 * TILE : (n // 2 + 1) * TILE],
            )
        )
    loads = [
        pltpu.make_async_copy(src, dst, load_sem.at[i]) for i, (src, dst) in enumerate(pairs)
    ]
    def greet_both(w):
        greet((w, me_n))
        greet((w, core_narrow))

    each_peer(greet_both)
    greet(core_peer)
    greet(x_peer)
    for load in loads:
        load.start()

    def remote(src, dst, send, recv, device):
        return pltpu.make_async_remote_copy(
            src_ref=src, dst_ref=dst, send_sem=send, recv_sem=recv,
            device_id=device, device_id_type=MESH,
        )

    loads[0].wait()
    child_rows = cmap[...]

    def order_group(g):
        first = g * GROUP
        low = (iota((2 * GROUP, 1), 0) + first) * rows
        chosen = (child_rows >= low) & (child_rows < low + rows)
        ones = jnp.where(chosen, 1.0, 0.0)
        before = []
        step = min(kids, 256)
        for start in range(0, kids, step):
            upper = iota((kids, step), 0) < iota((kids, step), 1) + start
            before.append(
                jnp.dot(
                    ones.astype(BF16),
                    jnp.where(upper, 1.0, 0.0).astype(BF16),
                    preferred_element_type=F32,
                )
            )
        rank = before[0] if len(before) == 1 else jnp.concatenate(before, axis=1)
        rank = jnp.where(chosen, rank, -1.0)
        wanted = iota((per_peer, kids), 0).astype(F32)
        base = jnp.zeros((1, kids), jnp.int32)
        for w in range(GROUP):
            here = rank[w : w + 1, :]
            pick[block_at(first + w, per_peer), :] = jnp.where(here == wanted, 1.0, 0.0).astype(BF16)
            base = jnp.where(here >= 0.0, (first + w) * rows, base)
        local = child_rows - base
        high = (local >> 4).astype(F32)
        less = (local & 15).astype(F32)
        line = iota((TILE, kids), 0)
        coded = jnp.where(line == 0, high, jnp.where(line == 1, less, 0.0)).astype(BF16)
        places = lax.dot_general(
            pick[block_at(g, slots), :], coded, (((1,), (1,)), ((), ())), preferred_element_type=F32
        ).astype(BF16)
        msg_out[pl.ds(first, GROUP), :per_peer, :] = places.reshape(GROUP, per_peer, TILE)

    def sort_group(g, source):
        sorted_rows[block_at(g, slots), source * touched : (source + 1) * touched] = jnp.dot(
            pick[block_at(g, slots), :], child[source], preferred_element_type=F32
        ).astype(BF16)

    repeat(groups, order_group)

    loads[1].wait()
    mask_pad[...] = jnp.zeros(mask_pad.shape, BF16)
    mask_pad[: mask.shape[0], : mask.shape[1]] = mask[...].astype(F32).astype(BF16)
    my_mask = mask_pad[...]
    repeat(groups, lambda g: msg_out.__setitem__(
        (pl.ds(g * GROUP, GROUP), slice(per_peer, per_peer + mask_rows)),
        jnp.broadcast_to(my_mask[None], (GROUP, mask_rows, TILE)),
    ))

    loads[2].wait()
    repeat(groups, lambda g: sort_group(g, 0))

    part = 384 if rows % 384 == 0 else rows

    def parent_mask(i):
        at = iota((part, mask_rows), 0) + i * part
        tile = iota((part, mask_rows), 1) * row_tile
        spread = jnp.where((at >= tile) & (at < tile + row_tile), 1.0, 0.0).astype(BF16)
        kept = jnp.dot(spread, my_mask, preferred_element_type=F32).astype(BF16)
        here = block_at(i, part)
        for t in range(cols // TILE):
            span = slice(t * TILE, (t + 1) * TILE)
            parent[here, span] = parent[here, span] * kept[:, t : t + 1]

    def parent_half(half):
        def one(i):
            product = jnp.dot(
                parent[block_at(i, part), :], probes[half], preferred_element_type=F32
            ).astype(BF16)
            for x in range(2):
                f_own[half, x, block_at(i, part), :] = product[:, x * TILE : (x + 1) * TILE]

        repeat(rows // part, one)

    loads[3].wait()
    repeat(rows // part, parent_mask)
    for load in loads[4:]:
        load.wait()
    parent_half(1 - core)

    pl.semaphore_wait(barrier, 2 * wide)
    pl.semaphore_signal(ready, inc=1, device_id=x_peer, device_id_type=MESH)

    far_copies = [remote(child_in, child.at[1], far_sem.at[0], far_sem.at[1], core_peer)]
    for x in range(2):
        span = pl.ds(pl.multiple_of((2 * x + 1 - core) * TILE, TILE), TILE)
        far_copies.append(
            remote(
                probes_in.at[:touched, span], probes_far.at[:, x * TILE : (x + 1) * TILE],
                far_sem.at[2 + 2 * x], far_sem.at[3 + 2 * x], core_peer,
            )
        )

    def tell_mask(w):
        remote(mask_pad, mask_far.at[me_w], msg_sem.at[2], msg_sem.at[3], (w, core_narrow)).start()

    def tell(w):
        remote(msg_out.at[w], msg_in.at[me_w], msg_sem.at[0], msg_sem.at[1], (w, me_n)).start()
        tell_mask(w)

    each_peer(tell)
    tell_mask(me_w)
    for copy in far_copies:
        copy.start()
    msg_in[me_w] = msg_out[me_w]
    masks = remote(mask_far, mask_far, msg_sem.at[2], msg_sem.at[3], core_peer)
    messages = remote(
        msg_out.at[pl.ds(0, wide - 1)], msg_in.at[pl.ds(0, wide - 1)],
        msg_sem.at[0], msg_sem.at[1], x_peer,
    )

    f_pair = remote(f_own.at[1 - core], f_core, pair_send.at[0], pair_recv.at[0], core_peer)
    f_pair.start()
    parent_half(core)
    far_copies[0].wait_recv()
    repeat(groups, lambda g: sort_group(g, 1))

    shift = mask_rows.bit_length() - 1

    def landing(g):
        place = msg_out[pl.ds(g * GROUP, GROUP), :per_peer, :].reshape(slots, TILE).astype(F32)
        place = place[:, 0:1] * 16.0 + place[:, 1:2]
        lane = iota((slots, GROUP * mask_rows), 1)
        peer = iota((slots, GROUP * mask_rows), 0) >> (per_peer.bit_length() - 1)
        tile = ((lane & (mask_rows - 1)) * row_tile).astype(F32)
        same = ((lane >> shift) == peer) & (place >= tile) & (place < tile + row_tile)
        return jnp.where(same, 1.0, 0.0).astype(BF16)

    def child_mask(g, tiles):
        table = msg_in[pl.ds(g * GROUP, GROUP), per_peer:, :].reshape(GROUP * mask_rows, TILE)
        far = mask_far[pl.ds(g * GROUP, GROUP)].reshape(GROUP * mask_rows, TILE)
        here = block_at(g, slots)
        count = touched // TILE
        for source, part_table in enumerate((table, far)):
            kept = jnp.dot(tiles, part_table, preferred_element_type=F32).astype(BF16)
            for t in range(count):
                span = slice((source * count + t) * TILE, (source * count + t + 1) * TILE)
                sorted_rows[here, span] = sorted_rows[here, span] * kept[:, t : t + 1]

    def child_product(g):
        here = block_at(g, slots)
        product = jnp.dot(
            sorted_rows[here, :touched], probes[core, :touched, :], preferred_element_type=F32
        ) + jnp.dot(sorted_rows[here, touched:], probes_far[...], preferred_element_type=F32)
        product = product.astype(BF16)
        for x in range(2):
            z_out[block_at(x * groups + g, slots), :] = product[:, x * TILE : (x + 1) * TILE]

    f_pair.wait_recv()
    f_send[...] = (f_own[core, 1 - along].astype(F32) + f_core[1 - along].astype(F32)).astype(BF16)
    f_cross = remote(f_send, f_x, pair_send.at[1], pair_recv.at[1], x_peer)
    f_cross.start()

    def all_in():
        messages.wait_recv()
        masks.wait_recv()

    def z_start(x, n, w):
        remote(
            z_out.at[block_at(x * wide + w, per_peer)],
            z_in.at[block_at(along * wide + me_w, per_peer)],
            z_sem.at[0], z_sem.at[1], (w, n),
        ).start()

    def z_both(w):
        z_start(1 - along, x_narrow, w)
        z_start(along, me_n, w)

    if groups == 1:
        count = touched // TILE
        tiles = landing(0)
        for copy in far_copies[1:]:
            copy.wait_recv()
        for t in range(2 * count):
            span = slice(t % count * TILE, (t % count + 1) * TILE)
            weights = probes_far[span, :] if t >= count else probes[core, span, :]
            tile_products[t] = jnp.dot(
                sorted_rows[:, t * TILE : (t + 1) * TILE], weights, preferred_element_type=F32
            )
        all_in()
        pl.semaphore_wait(ready, 1)
        kept = [
            jnp.dot(tiles, table.reshape(GROUP * mask_rows, TILE), preferred_element_type=F32)
            for table in (msg_in[:, per_peer:, :], mask_far[...])
        ]
        keep[0] = kept[0]
        keep[1] = kept[1]
        size = kids // 2
        for half, each in ((1 - my_half, each_far), (my_half, each_near)):
            here = block_at(half, size)
            product = jnp.zeros((size, 2 * TILE), F32)
            for t in range(2 * count):
                factor = keep[t // count, here, t % count : t % count + 1]
                product = product + factor * tile_products[t, here, :]
            product = product.astype(BF16)
            for x in range(2):
                z_out[block_at(x * 2 + half, size), :] = product[:, x * TILE : (x + 1) * TILE]
            each(z_both)
    else:
        all_in()
        repeat(groups, lambda g: child_mask(g, landing(g)))
        for copy in far_copies[1:]:
            copy.wait_recv()
        repeat(groups, child_product)
        pl.semaphore_wait(ready, 1)
        each_peer(z_both)
    z_start(1 - along, x_narrow, me_w)
    mine = block_at(along * wide + me_w, per_peer)
    z_in[mine, :] = z_out[mine, :]
    most = pl.ds(0, (2 * wide - 1) * per_peer)
    arrivals = remote(z_out.at[most], z_in.at[most], z_sem.at[0], z_sem.at[1], x_peer)

    for g in range(groups):
        place = msg_in[g * GROUP : (g + 1) * GROUP, :per_peer, :].reshape(slots, TILE)
        lane = iota((2 * GROUP, TILE), 1)
        weigh = jnp.where(lane == 0, 16.0, jnp.where(lane == 1, 1.0, 0.0)).astype(BF16)
        place = lax.dot_general(
            weigh, place, (((1,), (1,)), ((), ())), preferred_element_type=F32
        )[0:1, :]
        lands[:, g * slots : (g + 1) * slots] = jnp.where(
            place == iota((rows, slots), 0).astype(F32), 1.0, 0.0
        ).astype(BF16)
    f_cross.wait_recv()
    total = f_own[core, along].astype(F32) + f_core[along].astype(F32) + f_x[...].astype(F32)
    arrivals.wait_recv()
    both_chips = jnp.concatenate([z_in[:kids, :], z_in[kids:, :]], axis=1)
    added = jnp.dot(lands[...], both_chips, preferred_element_type=F32)
    out_ref[...] = (total + (added[:, :TILE] + added[:, TILE:])).astype(out_ref.dtype)

    messages.wait_send()
    masks.wait_send()
    arrivals.wait_send()
    for copy in (f_pair, f_cross, *far_copies):
        copy.wait_send()


def local(wide, narrow, parent_front, child_updates, child_map, tile_mask, probes):
    rows, cols = parent_front.shape
    kids, touched = child_updates.shape
    per_peer = kids // wide
    probe_cols = probes.shape[1]
    mask_rows = 16 * pl.cdiv(tile_mask.shape[0], 16)
    shapes = [
        ((rows, cols), BF16),
        ((2, kids, touched), BF16),
        ((1, kids), jnp.int32),
        (tile_mask.shape, jnp.int32),
        ((2, cols, 2 * TILE), BF16),
        ((mask_rows, TILE), BF16),
        ((touched, 2 * TILE), BF16),
        ((wide, per_peer + mask_rows, TILE), BF16),
        ((wide, per_peer + mask_rows, TILE), BF16),
        ((wide, mask_rows, TILE), BF16),
        ((kids, kids), BF16),
        ((kids, 2 * touched), BF16),
        ((rows, kids), BF16),
        ((2, 2, rows, TILE), BF16),
        ((2, rows, TILE), BF16),
        ((rows, TILE), BF16),
        ((rows, TILE), BF16),
        ((2 * kids, TILE), BF16),
        ((2 * kids, TILE), BF16),
        ((2 * touched // TILE, GROUP * per_peer, 2 * TILE), F32),
        ((2, GROUP * per_peer, TILE), F32),
    ]
    dma = pltpu.SemaphoreType.DMA
    return pl.pallas_call(
        functools.partial(kernel, wide, narrow, per_peer, mask_rows),
        out_shape=pltpu.VMEM((rows, probe_cols // narrow), BF16),
        in_specs=[pl.BlockSpec(memory_space=pltpu.HBM)] * 5,
        out_specs=pl.BlockSpec(memory_space=pltpu.VMEM),
        scratch_shapes=[pltpu.VMEM(shape, dtype) for shape, dtype in shapes]
        + [dma((8,)), dma((4,)), dma((6,)), dma((2,)), dma((2,)), dma((2,)), pltpu.SemaphoreType.REGULAR],
        compiler_params=pltpu.CompilerParams(
            collective_id=0, has_side_effects=True,
            vmem_limit_bytes=56 * 1024 * 1024,
        ),
    )(parent_front, child_updates, child_map.reshape(1, -1), tile_mask, probes)


def solution(mesh):
    placed = (
        P("wide", "narrow"),
        P("wide", "narrow"),
        P("wide"),
        P("wide", "narrow"),
        P("narrow", None),
    )
    return jax.shard_map(
        functools.partial(local, mesh.shape["wide"], mesh.shape["narrow"]),
        mesh=mesh, in_specs=placed, out_specs=P("wide", "narrow"), check_vma=False,
    )
```

```python
import functools

import jax
import jax.numpy as jnp
from jax import lax
from jax.experimental import pallas as pl
from jax.experimental.pallas import tpu as pltpu
from jax.sharding import PartitionSpec as P

TILE = 128
GROUP = 8
MESH = pl.DeviceIdType.MESH
F32 = jnp.float32
BF16 = jnp.bfloat16


def repeat(count, body):
    if count == 1:
        body(0)
    else:
        lax.fori_loop(0, count, lambda i, carry: (body(i), carry)[1], 0)


def iota(shape, dim):
    return lax.broadcasted_iota(jnp.int32, shape, dim)


def kernel(
    wide, narrow, per_peer, mask_rows,
    parent_in, child_in, map_in, mask_in, probes_in,
    out_ref,
    parent, child, cmap, mask, probes, mask_pad,
    probes_far, msg_out, msg_in, mask_far, pick, sorted_rows, lands,
    f_own, f_core, f_send, f_x,
    z_out, z_in, tile_products, keep,
    load_sem, msg_sem, far_sem, z_sem, pair_send, pair_recv, ready,
):
    rows, cols = parent.shape
    _, kids, touched = child.shape
    slots = GROUP * per_peer
    groups = wide // GROUP
    row_tile = rows // mask.shape[0]
    me_w = lax.axis_index("wide")
    me_n = lax.axis_index("narrow")
    core = lax.rem(me_n, 2)
    along = lax.div(me_n, 2)
    core_narrow = me_n + 1 - 2 * core
    core_peer = (me_w, core_narrow)
    x_narrow = lax.rem(me_n + 2, narrow)
    x_peer = (me_w, x_narrow)

    half_wide = wide // 2
    my_half = lax.div(me_w, half_wide)
    my_place = lax.rem(me_w, half_wide)

    def run(first, one):
        if wide <= GROUP:
            for k in range(first, half_wide):
                one(k)
        else:
            lax.fori_loop(first, half_wide, lambda k, carry: (one(k), carry)[1], 0)

    def each_far(fn):
        def one(k):
            fn((1 - my_half) * (wide - 1 - k) + my_half * k)

        run(0, one)

    def each_near(fn, first=1):
        def one(k):
            fn(my_half * half_wide + lax.rem(my_place + k, half_wide))

        run(first, one)

    def each_peer(fn):
        each_far(fn)
        each_near(fn)

    def block_at(index, size):
        return pl.ds(pl.multiple_of(index * size, size), size)

    barrier = pltpu.get_barrier_semaphore()

    def greet(device):
        pl.semaphore_signal(barrier, inc=1, device_id=device, device_id_type=MESH)

    pairs = [(map_in, cmap), (mask_in, mask), (child_in, child.at[0]), (parent_in, parent)]
    for n in range(narrow):
        pairs.append(
            (
                probes_in.at[:, n * TILE : (n + 1) * TILE],
                probes.at[n % 2, :, n // 2 * TILE : (n // 2 + 1) * TILE],
            )
        )
    loads = [
        pltpu.make_async_copy(src, dst, load_sem.at[i]) for i, (src, dst) in enumerate(pairs)
    ]
    def greet_both(w):
        greet((w, me_n))
        greet((w, core_narrow))

    each_peer(greet_both)
    greet(core_peer)
    greet(x_peer)
    for load in loads:
        load.start()

    def remote(src, dst, send, recv, device):
        return pltpu.make_async_remote_copy(
            src_ref=src, dst_ref=dst, send_sem=send, recv_sem=recv,
            device_id=device, device_id_type=MESH,
        )

    loads[0].wait()
    child_rows = cmap[...]

    def order_group(g):
        first = g * GROUP
        low = (iota((2 * GROUP, 1), 0) + first) * rows
        chosen = (child_rows >= low) & (child_rows < low + rows)
        ones = jnp.where(chosen, 1.0, 0.0)
        before = []
        step = min(kids, 256)
        for start in range(0, kids, step):
            upper = iota((kids, step), 0) < iota((kids, step), 1) + start
            before.append(
                jnp.dot(
                    ones.astype(BF16),
                    jnp.where(upper, 1.0, 0.0).astype(BF16),
                    preferred_element_type=F32,
                )
            )
        rank = before[0] if len(before) == 1 else jnp.concatenate(before, axis=1)
        rank = jnp.where(chosen, rank, -1.0)
        wanted = iota((per_peer, kids), 0).astype(F32)
        base = jnp.zeros((1, kids), jnp.int32)
        for w in range(GROUP):
            here = rank[w : w + 1, :]
            pick[block_at(first + w, per_peer), :] = jnp.where(here == wanted, 1.0, 0.0).astype(BF16)
            base = jnp.where(here >= 0.0, (first + w) * rows, base)
        local = child_rows - base
        high = (local >> 4).astype(F32)
        less = (local & 15).astype(F32)
        line = iota((TILE, kids), 0)
        coded = jnp.where(line == 0, high, jnp.where(line == 1, less, 0.0)).astype(BF16)
        places = lax.dot_general(
            pick[block_at(g, slots), :], coded, (((1,), (1,)), ((), ())), preferred_element_type=F32
        ).astype(BF16)
        msg_out[pl.ds(first, GROUP), :per_peer, :] = places.reshape(GROUP, per_peer, TILE)

    def sort_group(g, source):
        sorted_rows[block_at(g, slots), source * touched : (source + 1) * touched] = jnp.dot(
            pick[block_at(g, slots), :], child[source], preferred_element_type=F32
        ).astype(BF16)

    repeat(groups, order_group)

    loads[1].wait()
    mask_pad[...] = jnp.zeros(mask_pad.shape, BF16)
    mask_pad[: mask.shape[0], : mask.shape[1]] = mask[...].astype(F32).astype(BF16)
    my_mask = mask_pad[...]
    repeat(groups, lambda g: msg_out.__setitem__(
        (pl.ds(g * GROUP, GROUP), slice(per_peer, per_peer + mask_rows)),
        jnp.broadcast_to(my_mask[None], (GROUP, mask_rows, TILE)),
    ))

    loads[2].wait()
    repeat(groups, lambda g: sort_group(g, 0))

    part = 384 if rows % 384 == 0 else rows

    def parent_mask(i):
        at = iota((part, mask_rows), 0) + i * part
        tile = iota((part, mask_rows), 1) * row_tile
        spread = jnp.where((at >= tile) & (at < tile + row_tile), 1.0, 0.0).astype(BF16)
        kept = jnp.dot(spread, my_mask, preferred_element_type=F32).astype(BF16)
        here = block_at(i, part)
        for t in range(cols // TILE):
            span = slice(t * TILE, (t + 1) * TILE)
            parent[here, span] = parent[here, span] * kept[:, t : t + 1]

    def parent_half(half):
        def one(i):
            product = jnp.dot(
                parent[block_at(i, part), :], probes[half], preferred_element_type=F32
            ).astype(BF16)
            for x in range(2):
                f_own[half, x, block_at(i, part), :] = product[:, x * TILE : (x + 1) * TILE]

        repeat(rows // part, one)

    loads[3].wait()
    repeat(rows // part, parent_mask)
    for load in loads[4:]:
        load.wait()
    parent_half(1 - core)

    pl.semaphore_wait(barrier, 2 * wide)
    pl.semaphore_signal(ready, inc=1, device_id=x_peer, device_id_type=MESH)

    far_copies = [remote(child_in, child.at[1], far_sem.at[0], far_sem.at[1], core_peer)]
    for x in range(2):
        span = pl.ds(pl.multiple_of((2 * x + 1 - core) * TILE, TILE), TILE)
        far_copies.append(
            remote(
                probes_in.at[:touched, span], probes_far.at[:, x * TILE : (x + 1) * TILE],
                far_sem.at[2 + 2 * x], far_sem.at[3 + 2 * x], core_peer,
            )
        )

    def tell_mask(w):
        remote(mask_pad, mask_far.at[me_w], msg_sem.at[2], msg_sem.at[3], (w, core_narrow)).start()

    def tell(w):
        remote(msg_out.at[w], msg_in.at[me_w], msg_sem.at[0], msg_sem.at[1], (w, me_n)).start()
        tell_mask(w)

    each_peer(tell)
    tell_mask(me_w)
    for copy in far_copies:
        copy.start()
    msg_in[me_w] = msg_out[me_w]
    masks = remote(mask_far, mask_far, msg_sem.at[2], msg_sem.at[3], core_peer)
    messages = remote(
        msg_out.at[pl.ds(0, wide - 1)], msg_in.at[pl.ds(0, wide - 1)],
        msg_sem.at[0], msg_sem.at[1], x_peer,
    )

    f_pair = remote(f_own.at[1 - core], f_core, pair_send.at[0], pair_recv.at[0], core_peer)
    f_pair.start()
    parent_half(core)
    far_copies[0].wait_recv()
    repeat(groups, lambda g: sort_group(g, 1))

    shift = mask_rows.bit_length() - 1

    def landing(g):
        place = msg_out[pl.ds(g * GROUP, GROUP), :per_peer, :].reshape(slots, TILE).astype(F32)
        place = place[:, 0:1] * 16.0 + place[:, 1:2]
        lane = iota((slots, GROUP * mask_rows), 1)
        peer = iota((slots, GROUP * mask_rows), 0) >> (per_peer.bit_length() - 1)
        tile = ((lane & (mask_rows - 1)) * row_tile).astype(F32)
        same = ((lane >> shift) == peer) & (place >= tile) & (place < tile + row_tile)
        return jnp.where(same, 1.0, 0.0).astype(BF16)

    def child_mask(g, tiles):
        table = msg_in[pl.ds(g * GROUP, GROUP), per_peer:, :].reshape(GROUP * mask_rows, TILE)
        far = mask_far[pl.ds(g * GROUP, GROUP)].reshape(GROUP * mask_rows, TILE)
        here = block_at(g, slots)
        count = touched // TILE
        for source, part_table in enumerate((table, far)):
            kept = jnp.dot(tiles, part_table, preferred_element_type=F32).astype(BF16)
            for t in range(count):
                span = slice((source * count + t) * TILE, (source * count + t + 1) * TILE)
                sorted_rows[here, span] = sorted_rows[here, span] * kept[:, t : t + 1]

    def child_product(g):
        here = block_at(g, slots)
        product = jnp.dot(
            sorted_rows[here, :touched], probes[core, :touched, :], preferred_element_type=F32
        ) + jnp.dot(sorted_rows[here, touched:], probes_far[...], preferred_element_type=F32)
        product = product.astype(BF16)
        for x in range(2):
            z_out[block_at(x * groups + g, slots), :] = product[:, x * TILE : (x + 1) * TILE]

    f_pair.wait_recv()
    f_send[...] = (f_own[core, 1 - along].astype(F32) + f_core[1 - along].astype(F32)).astype(BF16)
    f_cross = remote(f_send, f_x, pair_send.at[1], pair_recv.at[1], x_peer)
    f_cross.start()

    def all_in():
        messages.wait_recv()
        masks.wait_recv()

    def z_start(x, n, w):
        remote(
            z_out.at[block_at(x * wide + w, per_peer)],
            z_in.at[block_at(along * wide + me_w, per_peer)],
            z_sem.at[0], z_sem.at[1], (w, n),
        ).start()

    def z_both(w):
        z_start(1 - along, x_narrow, w)
        z_start(along, me_n, w)

    if groups == 1:
        count = touched // TILE
        tiles = landing(0)
        for copy in far_copies[1:]:
            copy.wait_recv()
        for t in range(2 * count):
            span = slice(t % count * TILE, (t % count + 1) * TILE)
            weights = probes_far[span, :] if t >= count else probes[core, span, :]
            tile_products[t] = jnp.dot(
                sorted_rows[:, t * TILE : (t + 1) * TILE], weights, preferred_element_type=F32
            )
        all_in()
        pl.semaphore_wait(ready, 1)
        kept = [
            jnp.dot(tiles, table.reshape(GROUP * mask_rows, TILE), preferred_element_type=F32)
            for table in (msg_in[:, per_peer:, :], mask_far[...])
        ]
        keep[0] = kept[0]
        keep[1] = kept[1]

        def z_block(w):
            here = block_at(w, per_peer)
            product = jnp.zeros((per_peer, 2 * TILE), F32)
            for t in range(2 * count):
                factor = keep[t // count, here, t % count : t % count + 1]
                product = product + factor * tile_products[t, here, :]
            product = product.astype(BF16)
            for x in range(2):
                z_out[block_at(x * wide + w, per_peer), :] = product[:, x * TILE : (x + 1) * TILE]

        def z_blocks(w):
            z_block(w)
            z_start(core, 3 * core, w)
            z_start(1 - core, 2 - core, w)

        for k in range(half_wide):
            low = k + core * (half_wide - 1 - 2 * k)
            z_blocks((1 - my_half) * (wide - 1 - k) + my_half * low)
        each_near(z_blocks)
        z_block(me_w)
    else:
        all_in()
        repeat(groups, lambda g: child_mask(g, landing(g)))
        for copy in far_copies[1:]:
            copy.wait_recv()
        repeat(groups, child_product)
        pl.semaphore_wait(ready, 1)
        each_peer(z_both)
    z_start(1 - along, x_narrow, me_w)
    mine = block_at(along * wide + me_w, per_peer)
    z_in[mine, :] = z_out[mine, :]
    most = pl.ds(0, (2 * wide - 1) * per_peer)
    arrivals = remote(z_out.at[most], z_in.at[most], z_sem.at[0], z_sem.at[1], x_peer)

    for g in range(groups):
        place = msg_in[g * GROUP : (g + 1) * GROUP, :per_peer, :].reshape(slots, TILE)
        lane = iota((2 * GROUP, TILE), 1)
        weigh = jnp.where(lane == 0, 16.0, jnp.where(lane == 1, 1.0, 0.0)).astype(BF16)
        place = lax.dot_general(
            weigh, place, (((1,), (1,)), ((), ())), preferred_element_type=F32
        )[0:1, :]
        lands[:, g * slots : (g + 1) * slots] = jnp.where(
            place == iota((rows, slots), 0).astype(F32), 1.0, 0.0
        ).astype(BF16)
    f_cross.wait_recv()
    total = f_own[core, along].astype(F32) + f_core[along].astype(F32) + f_x[...].astype(F32)
    arrivals.wait_recv()
    both_chips = jnp.concatenate([z_in[:kids, :], z_in[kids:, :]], axis=1)
    added = jnp.dot(lands[...], both_chips, preferred_element_type=F32)
    out_ref[...] = (total + (added[:, :TILE] + added[:, TILE:])).astype(out_ref.dtype)

    messages.wait_send()
    masks.wait_send()
    arrivals.wait_send()
    for copy in (f_pair, f_cross, *far_copies):
        copy.wait_send()


def local(wide, narrow, parent_front, child_updates, child_map, tile_mask, probes):
    rows, cols = parent_front.shape
    kids, touched = child_updates.shape
    per_peer = kids // wide
    probe_cols = probes.shape[1]
    mask_rows = 16 * pl.cdiv(tile_mask.shape[0], 16)
    shapes = [
        ((rows, cols), BF16),
        ((2, kids, touched), BF16),
        ((1, kids), jnp.int32),
        (tile_mask.shape, jnp.int32),
        ((2, cols, 2 * TILE), BF16),
        ((mask_rows, TILE), BF16),
        ((touched, 2 * TILE), BF16),
        ((wide, per_peer + mask_rows, TILE), BF16),
        ((wide, per_peer + mask_rows, TILE), BF16),
        ((wide, mask_rows, TILE), BF16),
        ((kids, kids), BF16),
        ((kids, 2 * touched), BF16),
        ((rows, kids), BF16),
        ((2, 2, rows, TILE), BF16),
        ((2, rows, TILE), BF16),
        ((rows, TILE), BF16),
        ((rows, TILE), BF16),
        ((2 * kids, TILE), BF16),
        ((2 * kids, TILE), BF16),
        ((2 * touched // TILE, GROUP * per_peer, 2 * TILE), F32),
        ((2, GROUP * per_peer, TILE), F32),
    ]
    dma = pltpu.SemaphoreType.DMA
    return pl.pallas_call(
        functools.partial(kernel, wide, narrow, per_peer, mask_rows),
        out_shape=pltpu.VMEM((rows, probe_cols // narrow), BF16),
        in_specs=[pl.BlockSpec(memory_space=pltpu.HBM)] * 5,
        out_specs=pl.BlockSpec(memory_space=pltpu.VMEM),
        scratch_shapes=[pltpu.VMEM(shape, dtype) for shape, dtype in shapes]
        + [dma((8,)), dma((4,)), dma((6,)), dma((2,)), dma((2,)), dma((2,)), pltpu.SemaphoreType.REGULAR],
        compiler_params=pltpu.CompilerParams(
            collective_id=0, has_side_effects=True,
            vmem_limit_bytes=56 * 1024 * 1024,
        ),
    )(parent_front, child_updates, child_map.reshape(1, -1), tile_mask, probes)


def solution(mesh):
    placed = (
        P("wide", "narrow"),
        P("wide", "narrow"),
        P("wide"),
        P("wide", "narrow"),
        P("narrow", None),
    )
    return jax.shard_map(
        functools.partial(local, mesh.shape["wide"], mesh.shape["narrow"]),
        mesh=mesh, in_specs=placed, out_specs=P("wide", "narrow"), check_vma=False,
    )
```

```python
import functools

import jax
import jax.numpy as jnp
from jax import lax
from jax.experimental import pallas as pl
from jax.experimental.pallas import tpu as pltpu
from jax.sharding import PartitionSpec as P

TILE = 128
GROUP = 8
MESH = pl.DeviceIdType.MESH
F32 = jnp.float32
BF16 = jnp.bfloat16


def repeat(count, body):
    if count == 1:
        body(0)
    else:
        lax.fori_loop(0, count, lambda i, carry: (body(i), carry)[1], 0)


def iota(shape, dim):
    return lax.broadcasted_iota(jnp.int32, shape, dim)


def kernel(
    wide, narrow, per_peer, mask_rows,
    parent_in, child_in, map_in, mask_in, probes_in,
    out_ref,
    parent, child, cmap, mask, probes, mask_pad,
    probes_far, msg_out, msg_in, mask_far, pick, sorted_rows, lands,
    f_own, f_core, f_send, f_x,
    z_out, z_in, tile_products, keep,
    load_sem, msg_sem, far_sem, z_sem, pair_send, pair_recv, ready,
):
    rows, cols = parent.shape
    _, kids, touched = child.shape
    slots = GROUP * per_peer
    groups = wide // GROUP
    row_tile = rows // mask.shape[0]
    me_w = lax.axis_index("wide")
    me_n = lax.axis_index("narrow")
    core = lax.rem(me_n, 2)
    along = lax.div(me_n, 2)
    core_narrow = me_n + 1 - 2 * core
    core_peer = (me_w, core_narrow)
    x_narrow = lax.rem(me_n + 2, narrow)
    x_peer = (me_w, x_narrow)

    half_wide = wide // 2
    my_half = lax.div(me_w, half_wide)
    my_place = lax.rem(me_w, half_wide)

    def run(first, one):
        if wide <= GROUP:
            for k in range(first, half_wide):
                one(k)
        else:
            lax.fori_loop(first, half_wide, lambda k, carry: (one(k), carry)[1], 0)

    def each_far(fn):
        def one(k):
            fn((1 - my_half) * (wide - 1 - k) + my_half * k)

        run(0, one)

    def each_near(fn, first=1):
        def one(k):
            fn(my_half * half_wide + lax.rem(my_place + k, half_wide))

        run(first, one)

    def each_peer(fn):
        each_far(fn)
        each_near(fn)

    def block_at(index, size):
        return pl.ds(pl.multiple_of(index * size, size), size)

    barrier = pltpu.get_barrier_semaphore()

    def greet(device):
        pl.semaphore_signal(barrier, inc=1, device_id=device, device_id_type=MESH)

    pairs = [(map_in, cmap), (mask_in, mask), (child_in, child.at[0]), (parent_in, parent)]
    for n in range(narrow):
        pairs.append(
            (
                probes_in.at[:, n * TILE : (n + 1) * TILE],
                probes.at[n % 2, :, n // 2 * TILE : (n // 2 + 1) * TILE],
            )
        )
    loads = [
        pltpu.make_async_copy(src, dst, load_sem.at[i]) for i, (src, dst) in enumerate(pairs)
    ]
    def greet_both(w):
        greet((w, me_n))
        greet((w, core_narrow))

    each_peer(greet_both)
    greet(core_peer)
    greet(x_peer)
    for load in loads:
        load.start()

    def remote(src, dst, send, recv, device):
        return pltpu.make_async_remote_copy(
            src_ref=src, dst_ref=dst, send_sem=send, recv_sem=recv,
            device_id=device, device_id_type=MESH,
        )

    loads[0].wait()
    child_rows = cmap[...]

    def order_group(g):
        first = g * GROUP
        low = (iota((2 * GROUP, 1), 0) + first) * rows
        chosen = (child_rows >= low) & (child_rows < low + rows)
        ones = jnp.where(chosen, 1.0, 0.0)
        before = []
        step = min(kids, 256)
        for start in range(0, kids, step):
            upper = iota((kids, step), 0) < iota((kids, step), 1) + start
            before.append(
                jnp.dot(
                    ones.astype(BF16),
                    jnp.where(upper, 1.0, 0.0).astype(BF16),
                    preferred_element_type=F32,
                )
            )
        rank = before[0] if len(before) == 1 else jnp.concatenate(before, axis=1)
        rank = jnp.where(chosen, rank, -1.0)
        wanted = iota((per_peer, kids), 0).astype(F32)
        base = jnp.zeros((1, kids), jnp.int32)
        for w in range(GROUP):
            here = rank[w : w + 1, :]
            pick[block_at(first + w, per_peer), :] = jnp.where(here == wanted, 1.0, 0.0).astype(BF16)
            base = jnp.where(here >= 0.0, (first + w) * rows, base)
        local = child_rows - base
        high = (local >> 4).astype(F32)
        less = (local & 15).astype(F32)
        line = iota((TILE, kids), 0)
        coded = jnp.where(line == 0, high, jnp.where(line == 1, less, 0.0)).astype(BF16)
        places = lax.dot_general(
            pick[block_at(g, slots), :], coded, (((1,), (1,)), ((), ())), preferred_element_type=F32
        ).astype(BF16)
        msg_out[pl.ds(first, GROUP), :per_peer, :] = places.reshape(GROUP, per_peer, TILE)

    def sort_group(g, source):
        sorted_rows[block_at(g, slots), source * touched : (source + 1) * touched] = jnp.dot(
            pick[block_at(g, slots), :], child[source], preferred_element_type=F32
        ).astype(BF16)

    repeat(groups, order_group)

    loads[1].wait()
    mask_pad[...] = jnp.zeros(mask_pad.shape, BF16)
    mask_pad[: mask.shape[0], : mask.shape[1]] = mask[...].astype(F32).astype(BF16)
    my_mask = mask_pad[...]
    repeat(groups, lambda g: msg_out.__setitem__(
        (pl.ds(g * GROUP, GROUP), slice(per_peer, per_peer + mask_rows)),
        jnp.broadcast_to(my_mask[None], (GROUP, mask_rows, TILE)),
    ))

    loads[2].wait()
    repeat(groups, lambda g: sort_group(g, 0))

    part = 384 if rows % 384 == 0 else rows

    def parent_mask(i):
        at = iota((part, mask_rows), 0) + i * part
        tile = iota((part, mask_rows), 1) * row_tile
        spread = jnp.where((at >= tile) & (at < tile + row_tile), 1.0, 0.0).astype(BF16)
        kept = jnp.dot(spread, my_mask, preferred_element_type=F32).astype(BF16)
        here = block_at(i, part)
        for t in range(cols // TILE):
            span = slice(t * TILE, (t + 1) * TILE)
            parent[here, span] = parent[here, span] * kept[:, t : t + 1]

    def parent_half(half):
        def one(i):
            product = jnp.dot(
                parent[block_at(i, part), :], probes[half], preferred_element_type=F32
            ).astype(BF16)
            for x in range(2):
                f_own[half, x, block_at(i, part), :] = product[:, x * TILE : (x + 1) * TILE]

        repeat(rows // part, one)

    loads[3].wait()
    repeat(rows // part, parent_mask)
    for load in loads[4:]:
        load.wait()
    parent_half(1 - core)

    pl.semaphore_wait(barrier, 2 * wide)
    pl.semaphore_signal(ready, inc=1, device_id=x_peer, device_id_type=MESH)

    far_copies = [remote(child_in, child.at[1], far_sem.at[0], far_sem.at[1], core_peer)]
    for x in range(2):
        span = pl.ds(pl.multiple_of((2 * x + 1 - core) * TILE, TILE), TILE)
        far_copies.append(
            remote(
                probes_in.at[:touched, span], probes_far.at[:, x * TILE : (x + 1) * TILE],
                far_sem.at[2 + 2 * x], far_sem.at[3 + 2 * x], core_peer,
            )
        )

    def tell_mask(w):
        remote(mask_pad, mask_far.at[me_w], msg_sem.at[2], msg_sem.at[3], (w, core_narrow)).start()

    def tell(w):
        remote(msg_out.at[w], msg_in.at[me_w], msg_sem.at[0], msg_sem.at[1], (w, me_n)).start()
        tell_mask(w)

    each_peer(tell)
    tell_mask(me_w)
    for copy in far_copies:
        copy.start()
    msg_in[me_w] = msg_out[me_w]
    masks = remote(mask_far, mask_far, msg_sem.at[2], msg_sem.at[3], core_peer)
    messages = remote(
        msg_out.at[pl.ds(0, wide - 1)], msg_in.at[pl.ds(0, wide - 1)],
        msg_sem.at[0], msg_sem.at[1], x_peer,
    )

    f_pair = remote(f_own.at[1 - core], f_core, pair_send.at[0], pair_recv.at[0], core_peer)
    f_pair.start()
    parent_half(core)
    far_copies[0].wait_recv()
    repeat(groups, lambda g: sort_group(g, 1))

    shift = mask_rows.bit_length() - 1

    def landing(g):
        place = msg_out[pl.ds(g * GROUP, GROUP), :per_peer, :].reshape(slots, TILE).astype(F32)
        place = place[:, 0:1] * 16.0 + place[:, 1:2]
        lane = iota((slots, GROUP * mask_rows), 1)
        peer = iota((slots, GROUP * mask_rows), 0) >> (per_peer.bit_length() - 1)
        tile = ((lane & (mask_rows - 1)) * row_tile).astype(F32)
        same = ((lane >> shift) == peer) & (place >= tile) & (place < tile + row_tile)
        return jnp.where(same, 1.0, 0.0).astype(BF16)

    def child_mask(g, tiles):
        table = msg_in[pl.ds(g * GROUP, GROUP), per_peer:, :].reshape(GROUP * mask_rows, TILE)
        far = mask_far[pl.ds(g * GROUP, GROUP)].reshape(GROUP * mask_rows, TILE)
        here = block_at(g, slots)
        count = touched // TILE
        for source, part_table in enumerate((table, far)):
            kept = jnp.dot(tiles, part_table, preferred_element_type=F32).astype(BF16)
            for t in range(count):
                span = slice((source * count + t) * TILE, (source * count + t + 1) * TILE)
                sorted_rows[here, span] = sorted_rows[here, span] * kept[:, t : t + 1]

    def child_product(g):
        here = block_at(g, slots)
        product = jnp.dot(
            sorted_rows[here, :touched], probes[core, :touched, :], preferred_element_type=F32
        ) + jnp.dot(sorted_rows[here, touched:], probes_far[...], preferred_element_type=F32)
        product = product.astype(BF16)
        for x in range(2):
            z_out[block_at(x * groups + g, slots), :] = product[:, x * TILE : (x + 1) * TILE]

    f_pair.wait_recv()
    f_send[...] = (f_own[core, 1 - along].astype(F32) + f_core[1 - along].astype(F32)).astype(BF16)
    f_cross = remote(f_send, f_x, pair_send.at[1], pair_recv.at[1], x_peer)
    f_cross.start()

    def all_in():
        messages.wait_recv()
        masks.wait_recv()

    def z_start(x, n, w):
        remote(
            z_out.at[block_at(x * wide + w, per_peer)],
            z_in.at[block_at(along * wide + me_w, per_peer)],
            z_sem.at[0], z_sem.at[1], (w, n),
        ).start()

    def z_both(w):
        z_start(1 - along, x_narrow, w)
        z_start(along, me_n, w)

    if groups == 1:
        count = touched // TILE
        tiles = landing(0)
        for copy in far_copies[1:]:
            copy.wait_recv()
        for t in range(2 * count):
            span = slice(t % count * TILE, (t % count + 1) * TILE)
            weights = probes_far[span, :] if t >= count else probes[core, span, :]
            tile_products[t] = jnp.dot(
                sorted_rows[:, t * TILE : (t + 1) * TILE], weights, preferred_element_type=F32
            )
        all_in()
        pl.semaphore_wait(ready, 1)
        kept = [
            jnp.dot(tiles, table.reshape(GROUP * mask_rows, TILE), preferred_element_type=F32)
            for table in (msg_in[:, per_peer:, :], mask_far[...])
        ]
        keep[0] = kept[0]
        keep[1] = kept[1]

        def z_block(w):
            here = block_at(w, per_peer)
            product = jnp.zeros((per_peer, 2 * TILE), F32)
            for t in range(2 * count):
                factor = keep[t // count, here, t % count : t % count + 1]
                product = product + factor * tile_products[t, here, :]
            product = product.astype(BF16)
            for x in range(2):
                z_out[block_at(x * wide + w, per_peer), :] = product[:, x * TILE : (x + 1) * TILE]

        def z_blocks(w):
            z_block(w)
            z_start(0, core, w)
            z_start(1, 2 + core, w)

        each_far(z_blocks)
        each_near(z_blocks)
        z_block(me_w)
    else:
        all_in()
        repeat(groups, lambda g: child_mask(g, landing(g)))
        for copy in far_copies[1:]:
            copy.wait_recv()
        repeat(groups, child_product)
        pl.semaphore_wait(ready, 1)
        each_peer(z_both)
    z_start(1 - along, x_narrow, me_w)
    mine = block_at(along * wide + me_w, per_peer)
    z_in[mine, :] = z_out[mine, :]
    most = pl.ds(0, (2 * wide - 1) * per_peer)
    arrivals = remote(z_out.at[most], z_in.at[most], z_sem.at[0], z_sem.at[1], x_peer)

    for g in range(groups):
        place = msg_in[g * GROUP : (g + 1) * GROUP, :per_peer, :].reshape(slots, TILE)
        lane = iota((2 * GROUP, TILE), 1)
        weigh = jnp.where(lane == 0, 16.0, jnp.where(lane == 1, 1.0, 0.0)).astype(BF16)
        place = lax.dot_general(
            weigh, place, (((1,), (1,)), ((), ())), preferred_element_type=F32
        )[0:1, :]
        lands[:, g * slots : (g + 1) * slots] = jnp.where(
            place == iota((rows, slots), 0).astype(F32), 1.0, 0.0
        ).astype(BF16)
    f_cross.wait_recv()
    total = f_own[core, along].astype(F32) + f_core[along].astype(F32) + f_x[...].astype(F32)
    arrivals.wait_recv()
    both_chips = jnp.concatenate([z_in[:kids, :], z_in[kids:, :]], axis=1)
    added = jnp.dot(lands[...], both_chips, preferred_element_type=F32)
    out_ref[...] = (total + (added[:, :TILE] + added[:, TILE:])).astype(out_ref.dtype)

    messages.wait_send()
    masks.wait_send()
    arrivals.wait_send()
    for copy in (f_pair, f_cross, *far_copies):
        copy.wait_send()


def local(wide, narrow, parent_front, child_updates, child_map, tile_mask, probes):
    rows, cols = parent_front.shape
    kids, touched = child_updates.shape
    per_peer = kids // wide
    probe_cols = probes.shape[1]
    mask_rows = 16 * pl.cdiv(tile_mask.shape[0], 16)
    shapes = [
        ((rows, cols), BF16),
        ((2, kids, touched), BF16),
        ((1, kids), jnp.int32),
        (tile_mask.shape, jnp.int32),
        ((2, cols, 2 * TILE), BF16),
        ((mask_rows, TILE), BF16),
        ((touched, 2 * TILE), BF16),
        ((wide, per_peer + mask_rows, TILE), BF16),
        ((wide, per_peer + mask_rows, TILE), BF16),
        ((wide, mask_rows, TILE), BF16),
        ((kids, kids), BF16),
        ((kids, 2 * touched), BF16),
        ((rows, kids), BF16),
        ((2, 2, rows, TILE), BF16),
        ((2, rows, TILE), BF16),
        ((rows, TILE), BF16),
        ((rows, TILE), BF16),
        ((2 * kids, TILE), BF16),
        ((2 * kids, TILE), BF16),
        ((2 * touched // TILE, GROUP * per_peer, 2 * TILE), F32),
        ((2, GROUP * per_peer, TILE), F32),
    ]
    dma = pltpu.SemaphoreType.DMA
    return pl.pallas_call(
        functools.partial(kernel, wide, narrow, per_peer, mask_rows),
        out_shape=pltpu.VMEM((rows, probe_cols // narrow), BF16),
        in_specs=[pl.BlockSpec(memory_space=pltpu.HBM)] * 5,
        out_specs=pl.BlockSpec(memory_space=pltpu.VMEM),
        scratch_shapes=[pltpu.VMEM(shape, dtype) for shape, dtype in shapes]
        + [dma((8,)), dma((4,)), dma((6,)), dma((2,)), dma((2,)), dma((2,)), pltpu.SemaphoreType.REGULAR],
        compiler_params=pltpu.CompilerParams(
            collective_id=0, has_side_effects=True,
            vmem_limit_bytes=56 * 1024 * 1024,
        ),
    )(parent_front, child_updates, child_map.reshape(1, -1), tile_mask, probes)


def solution(mesh):
    placed = (
        P("wide", "narrow"),
        P("wide", "narrow"),
        P("wide"),
        P("wide", "narrow"),
        P("narrow", None),
    )
    return jax.shard_map(
        functools.partial(local, mesh.shape["wide"], mesh.shape["narrow"]),
        mesh=mesh, in_specs=placed, out_specs=P("wide", "narrow"), check_vma=False,
    )
```

```python
import functools

import jax
import jax.numpy as jnp
from jax import lax
from jax.experimental import pallas as pl
from jax.experimental.pallas import tpu as pltpu
from jax.sharding import PartitionSpec as P

TILE = 128
GROUP = 8
MESH = pl.DeviceIdType.MESH
F32 = jnp.float32
BF16 = jnp.bfloat16


def repeat(count, body):
    if count == 1:
        body(0)
    else:
        lax.fori_loop(0, count, lambda i, carry: (body(i), carry)[1], 0)


def iota(shape, dim):
    return lax.broadcasted_iota(jnp.int32, shape, dim)


def kernel(
    wide, narrow, per_peer, mask_rows,
    parent_in, child_in, map_in, mask_in, probes_in,
    out_ref,
    parent, child, cmap, mask, probes, mask_pad,
    probes_far, msg_out, msg_in, mask_far, pick, sorted_rows, lands,
    f_own, f_core, f_send, f_x,
    z_out, z_in, tile_products, keep,
    load_sem, msg_sem, far_sem, z_sem, pair_send, pair_recv, ready,
):
    rows, cols = parent.shape
    _, kids, touched = child.shape
    slots = GROUP * per_peer
    groups = wide // GROUP
    row_tile = rows // mask.shape[0]
    me_w = lax.axis_index("wide")
    me_n = lax.axis_index("narrow")
    core = lax.rem(me_n, 2)
    along = lax.div(me_n, 2)
    core_narrow = me_n + 1 - 2 * core
    core_peer = (me_w, core_narrow)
    x_narrow = lax.rem(me_n + 2, narrow)
    x_peer = (me_w, x_narrow)

    half_wide = wide // 2
    my_half = lax.div(me_w, half_wide)
    my_place = lax.rem(me_w, half_wide)

    def run(first, one):
        if wide <= GROUP:
            for k in range(first, half_wide):
                one(k)
        else:
            lax.fori_loop(first, half_wide, lambda k, carry: (one(k), carry)[1], 0)

    def each_far(fn):
        def one(k):
            fn((1 - my_half) * (wide - 1 - k) + my_half * k)

        run(0, one)

    def each_near(fn, first=1):
        def one(k):
            fn(my_half * half_wide + lax.rem(my_place + k, half_wide))

        run(first, one)

    def each_peer(fn):
        each_far(fn)
        each_near(fn)

    def block_at(index, size):
        return pl.ds(pl.multiple_of(index * size, size), size)

    barrier = pltpu.get_barrier_semaphore()

    def greet(device):
        pl.semaphore_signal(barrier, inc=1, device_id=device, device_id_type=MESH)

    pairs = [(map_in, cmap), (mask_in, mask), (child_in, child.at[0]), (parent_in, parent)]
    for n in range(narrow):
        pairs.append(
            (
                probes_in.at[:, n * TILE : (n + 1) * TILE],
                probes.at[n % 2, :, n // 2 * TILE : (n // 2 + 1) * TILE],
            )
        )
    loads = [
        pltpu.make_async_copy(src, dst, load_sem.at[i]) for i, (src, dst) in enumerate(pairs)
    ]
    def greet_both(w):
        greet((w, me_n))
        greet((w, core_narrow))

    each_peer(greet_both)
    greet(core_peer)
    greet(x_peer)
    for load in loads:
        load.start()

    def remote(src, dst, send, recv, device):
        return pltpu.make_async_remote_copy(
            src_ref=src, dst_ref=dst, send_sem=send, recv_sem=recv,
            device_id=device, device_id_type=MESH,
        )

    loads[0].wait()
    child_rows = cmap[...]

    def order_group(g):
        first = g * GROUP
        low = (iota((2 * GROUP, 1), 0) + first) * rows
        chosen = (child_rows >= low) & (child_rows < low + rows)
        ones = jnp.where(chosen, 1.0, 0.0)
        before = []
        step = min(kids, 256)
        for start in range(0, kids, step):
            upper = iota((kids, step), 0) < iota((kids, step), 1) + start
            before.append(
                jnp.dot(
                    ones.astype(BF16),
                    jnp.where(upper, 1.0, 0.0).astype(BF16),
                    preferred_element_type=F32,
                )
            )
        rank = before[0] if len(before) == 1 else jnp.concatenate(before, axis=1)
        rank = jnp.where(chosen, rank, -1.0)
        wanted = iota((per_peer, kids), 0).astype(F32)
        base = jnp.zeros((1, kids), jnp.int32)
        for w in range(GROUP):
            here = rank[w : w + 1, :]
            pick[block_at(first + w, per_peer), :] = jnp.where(here == wanted, 1.0, 0.0).astype(BF16)
            base = jnp.where(here >= 0.0, (first + w) * rows, base)
        local = child_rows - base
        high = (local >> 4).astype(F32)
        less = (local & 15).astype(F32)
        line = iota((TILE, kids), 0)
        coded = jnp.where(line == 0, high, jnp.where(line == 1, less, 0.0)).astype(BF16)
        places = lax.dot_general(
            pick[block_at(g, slots), :], coded, (((1,), (1,)), ((), ())), preferred_element_type=F32
        ).astype(BF16)
        msg_out[pl.ds(first, GROUP), :per_peer, :] = places.reshape(GROUP, per_peer, TILE)

    def sort_group(g, source):
        sorted_rows[block_at(g, slots), source * touched : (source + 1) * touched] = jnp.dot(
            pick[block_at(g, slots), :], child[source], preferred_element_type=F32
        ).astype(BF16)

    repeat(groups, order_group)

    loads[1].wait()
    mask_pad[...] = jnp.zeros(mask_pad.shape, BF16)
    mask_pad[: mask.shape[0], : mask.shape[1]] = mask[...].astype(F32).astype(BF16)
    my_mask = mask_pad[...]
    repeat(groups, lambda g: msg_out.__setitem__(
        (pl.ds(g * GROUP, GROUP), slice(per_peer, per_peer + mask_rows)),
        jnp.broadcast_to(my_mask[None], (GROUP, mask_rows, TILE)),
    ))

    loads[2].wait()
    repeat(groups, lambda g: sort_group(g, 0))

    part = 384 if rows % 384 == 0 else rows

    def parent_mask(i):
        at = iota((part, mask_rows), 0) + i * part
        tile = iota((part, mask_rows), 1) * row_tile
        spread = jnp.where((at >= tile) & (at < tile + row_tile), 1.0, 0.0).astype(BF16)
        kept = jnp.dot(spread, my_mask, preferred_element_type=F32).astype(BF16)
        here = block_at(i, part)
        for t in range(cols // TILE):
            span = slice(t * TILE, (t + 1) * TILE)
            parent[here, span] = parent[here, span] * kept[:, t : t + 1]

    def parent_half(half):
        def one(i):
            product = jnp.dot(
                parent[block_at(i, part), :], probes[half], preferred_element_type=F32
            ).astype(BF16)
            for x in range(2):
                f_own[half, x, block_at(i, part), :] = product[:, x * TILE : (x + 1) * TILE]

        repeat(rows // part, one)

    loads[3].wait()
    repeat(rows // part, parent_mask)
    for load in loads[4:]:
        load.wait()
    parent_half(1 - core)

    pl.semaphore_wait(barrier, 2 * wide)
    pl.semaphore_signal(ready, inc=1, device_id=x_peer, device_id_type=MESH)

    far_copies = [remote(child_in, child.at[1], far_sem.at[0], far_sem.at[1], core_peer)]
    for x in range(2):
        span = pl.ds(pl.multiple_of((2 * x + 1 - core) * TILE, TILE), TILE)
        far_copies.append(
            remote(
                probes_in.at[:touched, span], probes_far.at[:, x * TILE : (x + 1) * TILE],
                far_sem.at[2 + 2 * x], far_sem.at[3 + 2 * x], core_peer,
            )
        )

    def tell_mask(w):
        remote(mask_pad, mask_far.at[me_w], msg_sem.at[2], msg_sem.at[3], (w, core_narrow)).start()

    def tell(w):
        remote(msg_out.at[w], msg_in.at[me_w], msg_sem.at[0], msg_sem.at[1], (w, me_n)).start()
        tell_mask(w)

    each_peer(tell)
    tell_mask(me_w)
    for copy in far_copies:
        copy.start()
    msg_in[me_w] = msg_out[me_w]
    masks = remote(mask_far, mask_far, msg_sem.at[2], msg_sem.at[3], core_peer)
    messages = remote(
        msg_out.at[pl.ds(0, wide - 1)], msg_in.at[pl.ds(0, wide - 1)],
        msg_sem.at[0], msg_sem.at[1], x_peer,
    )

    f_pair = remote(f_own.at[1 - core], f_core, pair_send.at[0], pair_recv.at[0], core_peer)
    f_pair.start()
    parent_half(core)
    far_copies[0].wait_recv()
    repeat(groups, lambda g: sort_group(g, 1))

    shift = mask_rows.bit_length() - 1

    def landing(g):
        place = msg_out[pl.ds(g * GROUP, GROUP), :per_peer, :].reshape(slots, TILE).astype(F32)
        place = place[:, 0:1] * 16.0 + place[:, 1:2]
        lane = iota((slots, GROUP * mask_rows), 1)
        peer = iota((slots, GROUP * mask_rows), 0) >> (per_peer.bit_length() - 1)
        tile = ((lane & (mask_rows - 1)) * row_tile).astype(F32)
        same = ((lane >> shift) == peer) & (place >= tile) & (place < tile + row_tile)
        return jnp.where(same, 1.0, 0.0).astype(BF16)

    def child_mask(g, tiles):
        table = msg_in[pl.ds(g * GROUP, GROUP), per_peer:, :].reshape(GROUP * mask_rows, TILE)
        far = mask_far[pl.ds(g * GROUP, GROUP)].reshape(GROUP * mask_rows, TILE)
        here = block_at(g, slots)
        count = touched // TILE
        for source, part_table in enumerate((table, far)):
            kept = jnp.dot(tiles, part_table, preferred_element_type=F32).astype(BF16)
            for t in range(count):
                span = slice((source * count + t) * TILE, (source * count + t + 1) * TILE)
                sorted_rows[here, span] = sorted_rows[here, span] * kept[:, t : t + 1]

    def child_product(g):
        here = block_at(g, slots)
        product = jnp.dot(
            sorted_rows[here, :touched], probes[core, :touched, :], preferred_element_type=F32
        ) + jnp.dot(sorted_rows[here, touched:], probes_far[...], preferred_element_type=F32)
        product = product.astype(BF16)
        for x in range(2):
            z_out[block_at(x * groups + g, slots), :] = product[:, x * TILE : (x + 1) * TILE]

    f_cross = remote(f_send, f_x, pair_send.at[1], pair_recv.at[1], x_peer)

    def send_parent():
        f_pair.wait_recv()
        f_send[...] = (f_own[core, 1 - along].astype(F32) + f_core[1 - along].astype(F32)).astype(BF16)
        f_cross.start()

    def all_in():
        messages.wait_recv()
        masks.wait_recv()

    def z_start(x, n, w):
        remote(
            z_out.at[block_at(x * wide + w, per_peer)],
            z_in.at[block_at(along * wide + me_w, per_peer)],
            z_sem.at[0], z_sem.at[1], (w, n),
        ).start()

    def z_both(w):
        z_start(1 - along, x_narrow, w)
        z_start(along, me_n, w)

    if groups == 1:
        count = touched // TILE
        tiles = landing(0)
        for copy in far_copies[1:]:
            copy.wait_recv()
        for t in range(2 * count):
            span = slice(t % count * TILE, (t % count + 1) * TILE)
            weights = probes_far[span, :] if t >= count else probes[core, span, :]
            tile_products[t] = jnp.dot(
                sorted_rows[:, t * TILE : (t + 1) * TILE], weights, preferred_element_type=F32
            )
        send_parent()
        all_in()
        pl.semaphore_wait(ready, 1)
        kept = [
            jnp.dot(tiles, table.reshape(GROUP * mask_rows, TILE), preferred_element_type=F32)
            for table in (msg_in[:, per_peer:, :], mask_far[...])
        ]
        keep[0] = kept[0]
        keep[1] = kept[1]

        def z_block(w):
            here = block_at(w, per_peer)
            product = jnp.zeros((per_peer, 2 * TILE), F32)
            for t in range(2 * count):
                factor = keep[t // count, here, t % count : t % count + 1]
                product = product + factor * tile_products[t, here, :]
            product = product.astype(BF16)
            for x in range(2):
                z_out[block_at(x * wide + w, per_peer), :] = product[:, x * TILE : (x + 1) * TILE]

        def z_blocks(w):
            z_block(w)
            z_start(0, core, w)
            z_start(1, 2 + core, w)

        each_far(z_blocks)
        each_near(z_blocks)
        z_block(me_w)
    else:
        send_parent()
        all_in()
        repeat(groups, lambda g: child_mask(g, landing(g)))
        for copy in far_copies[1:]:
            copy.wait_recv()
        repeat(groups, child_product)
        pl.semaphore_wait(ready, 1)
        each_peer(z_both)
    z_start(1 - along, x_narrow, me_w)
    mine = block_at(along * wide + me_w, per_peer)
    z_in[mine, :] = z_out[mine, :]
    most = pl.ds(0, (2 * wide - 1) * per_peer)
    arrivals = remote(z_out.at[most], z_in.at[most], z_sem.at[0], z_sem.at[1], x_peer)

    for g in range(groups):
        place = msg_in[g * GROUP : (g + 1) * GROUP, :per_peer, :].reshape(slots, TILE)
        lane = iota((2 * GROUP, TILE), 1)
        weigh = jnp.where(lane == 0, 16.0, jnp.where(lane == 1, 1.0, 0.0)).astype(BF16)
        place = lax.dot_general(
            weigh, place, (((1,), (1,)), ((), ())), preferred_element_type=F32
        )[0:1, :]
        lands[:, g * slots : (g + 1) * slots] = jnp.where(
            place == iota((rows, slots), 0).astype(F32), 1.0, 0.0
        ).astype(BF16)
    f_cross.wait_recv()
    total = f_own[core, along].astype(F32) + f_core[along].astype(F32) + f_x[...].astype(F32)
    arrivals.wait_recv()
    both_chips = jnp.concatenate([z_in[:kids, :], z_in[kids:, :]], axis=1)
    added = jnp.dot(lands[...], both_chips, preferred_element_type=F32)
    out_ref[...] = (total + (added[:, :TILE] + added[:, TILE:])).astype(out_ref.dtype)

    messages.wait_send()
    masks.wait_send()
    arrivals.wait_send()
    for copy in (f_pair, f_cross, *far_copies):
        copy.wait_send()


def local(wide, narrow, parent_front, child_updates, child_map, tile_mask, probes):
    rows, cols = parent_front.shape
    kids, touched = child_updates.shape
    per_peer = kids // wide
    probe_cols = probes.shape[1]
    mask_rows = 16 * pl.cdiv(tile_mask.shape[0], 16)
    shapes = [
        ((rows, cols), BF16),
        ((2, kids, touched), BF16),
        ((1, kids), jnp.int32),
        (tile_mask.shape, jnp.int32),
        ((2, cols, 2 * TILE), BF16),
        ((mask_rows, TILE), BF16),
        ((touched, 2 * TILE), BF16),
        ((wide, per_peer + mask_rows, TILE), BF16),
        ((wide, per_peer + mask_rows, TILE), BF16),
        ((wide, mask_rows, TILE), BF16),
        ((kids, kids), BF16),
        ((kids, 2 * touched), BF16),
        ((rows, kids), BF16),
        ((2, 2, rows, TILE), BF16),
        ((2, rows, TILE), BF16),
        ((rows, TILE), BF16),
        ((rows, TILE), BF16),
        ((2 * kids, TILE), BF16),
        ((2 * kids, TILE), BF16),
        ((2 * touched // TILE, GROUP * per_peer, 2 * TILE), F32),
        ((2, GROUP * per_peer, TILE), F32),
    ]
    dma = pltpu.SemaphoreType.DMA
    return pl.pallas_call(
        functools.partial(kernel, wide, narrow, per_peer, mask_rows),
        out_shape=pltpu.VMEM((rows, probe_cols // narrow), BF16),
        in_specs=[pl.BlockSpec(memory_space=pltpu.HBM)] * 5,
        out_specs=pl.BlockSpec(memory_space=pltpu.VMEM),
        scratch_shapes=[pltpu.VMEM(shape, dtype) for shape, dtype in shapes]
        + [dma((8,)), dma((4,)), dma((6,)), dma((2,)), dma((2,)), dma((2,)), pltpu.SemaphoreType.REGULAR],
        compiler_params=pltpu.CompilerParams(
            collective_id=0, has_side_effects=True,
            vmem_limit_bytes=56 * 1024 * 1024,
        ),
    )(parent_front, child_updates, child_map.reshape(1, -1), tile_mask, probes)


def solution(mesh):
    placed = (
        P("wide", "narrow"),
        P("wide", "narrow"),
        P("wide"),
        P("wide", "narrow"),
        P("narrow", None),
    )
    return jax.shard_map(
        functools.partial(local, mesh.shape["wide"], mesh.shape["narrow"]),
        mesh=mesh, in_specs=placed, out_specs=P("wide", "narrow"), check_vma=False,
    )
```
